256 devices in a mesh: row: 8 (over x, core), col: 8 (over y, z_lo), shard: 4 (over z_hi).
Axes of the slice: x: 4, y: 4, z: 8 (z_hi: 4, z_lo: 2; z = z_hi * 2 + z_lo), core: 2. Of those that a mesh axis runs over, the one named last changes fastest.
Arguments:
- tokens: bfloat16 [8, 8, 2048, 1024], P('row', 'col', 'shard'), may hold values from -6 to 6
- cotangent: bfloat16 [8, 8, 2048, 1024], P('row', 'col', 'shard'), may hold values from -6 to 6
- w_in: bfloat16 [8, 1024, 4096], P('row', 'shard'), may hold values from -0.1875 to 0.1875
- w_out: bfloat16 [8, 4096, 1024], P('col', None, 'shard'), may hold values from -0.09375 to 0.09375
- frag_index: int32 [16], replicated, may hold values from 0 to 3
- mom_in: float32 [8, 1024, 1024], P('row', 'shard'), may hold values from -4 to 4
- mom_out: float32 [8, 1024, 1024], P('col', None, 'shard'), may hold values from -4 to 4
Outputs:
- mixed: bfloat16 [8, 8, 2048, 1024], P('row', 'col', 'shard')
- new_in: bfloat16 [8, 1024, 1024], P('row', 'shard')
- new_mom_in: float32 [8, 1024, 1024], P('row', 'shard')
- new_out: bfloat16 [8, 1024, 1024], P('col', None, 'shard')
- new_mom_out: float32 [8, 1024, 1024], P('col', None, 'shard')
The draws below stay inside these ranges and needn't reach their ends.
Inputs may be any that keep to these rules, and one draw needn't show every extreme that they name: `frag_index`: one fragment index per level-1 module, followed by one per level-2 module.
All inputs are finite; a program needn't handle non-finite values.
Results may differ from the reference program's by a relative error of at most 0.0061.
Values may be sent and summed in bfloat16 or wider, within the bound.
A program may use at most 192 MiB of HBM per device.

```python
import jax
import jax.numpy as jnp
from jax import lax

D = 1024
F = 4096
FU = 1024
TOK_PATH = 2048
MOD1 = 8
MOD2 = 8
NFRAG = 4


def with_ends(result, stream_key, least, largest):
    place = [jax.random.randint(jax.random.fold_in(stream_key, axis), (), 0, length) for axis, length in enumerate(result.shape)]
    widest = result.shape.index(max(result.shape))
    next_to = place[:widest] + [(place[widest] + 1) % result.shape[widest]] + place[widest + 1:]
    return result.at[tuple(place)].set(least).at[tuple(next_to)].set(largest)


def level_of(own_key, dims, shards, least, top_value):
    def one(axis_at, blocks):
        draws = jax.random.uniform(jax.random.fold_in(jax.random.fold_in(own_key, 6), axis_at), (blocks,), jnp.float32, least / len(shards), top_value / len(shards))
        return jnp.repeat(jnp.exp(draws), dims[axis_at] // blocks).reshape((-1,) + (1,) * (len(dims) - axis_at - 1))

    level = one(*shards[0])
    for cut in shards[1:]:
        level = level * one(*cut)
    return level


def centred(key, shape, width, most, pieces=(), held_as=jnp.bfloat16):
    entries = jax.random.normal(key, shape, jnp.float32) * width
    if len(pieces) > 0:
        entries = level_of(key, shape, pieces, -0.22, 0.18) * entries
    return jnp.clip(entries, min=-most, max=most).astype(held_as)


def setup_inputs(seed: int = 0) -> dict:
    seeds = jax.random.split(jax.random.key(seed), 8)
    return {
        "tokens": centred(seeds[0], (MOD1, MOD2, TOK_PATH, D), 1.0, 6.0, ((0, 8), (1, 8), (2, 4))),
        "cotangent": centred(seeds[1], (MOD1, MOD2, TOK_PATH, D), 1.0, 6.0, ((0, 8), (1, 8), (2, 4))),
        "w_in": centred(seeds[2], (MOD1, D, F), D ** -0.5, 0.1875, ((0, 8), (1, 4))),
        "w_out": centred(seeds[3], (MOD2, F, D), F ** -0.5, 0.09375, ((0, 8), (2, 4))),
        "frag_index": with_ends(jax.random.randint(seeds[4], (MOD1 + MOD2,), 0, NFRAG), jax.random.fold_in(seeds[4], 1), 0, NFRAG - 1).astype(jnp.int32),
        "mom_in": centred(seeds[5], (MOD1, D, FU), 0.5, 4.0, ((0, 8), (1, 4)), jnp.float32),
        "mom_out": centred(seeds[6], (MOD2, FU, D), 0.5, 4.0, ((0, 8), (2, 4)), jnp.float32),
    }


EPS = 1e-06
INNER_LR = 0.05
MOMENTUM = 0.9
OUTER_LR = 0.7
GELU_SCALE = 0.7978845608028654
GELU_CUBIC = 0.044715

def gelu_parts(preact):
    tangent = jnp.tanh(GELU_SCALE * (preact + GELU_CUBIC * preact * preact * preact))
    value = 0.5 * preact * (1.0 + tangent)
    slope = 0.5 * (1.0 + tangent) + 0.5 * preact * (1.0 - tangent * tangent) * GELU_SCALE * (1.0 + 3.0 * GELU_CUBIC * preact * preact)
    return (value, slope)

def normalize(inputs):
    stream = inputs.astype(jnp.float32)
    normed = (stream * lax.rsqrt(lax.optimization_barrier(jnp.mean(stream * stream, axis=-1, keepdims=True)) + EPS)).astype(jnp.bfloat16)
    return (stream, normed)

def reference(tokens, cotangent, w_in, w_out, frag_index, mom_in, mom_out):
    starts_in = (frag_index[:MOD1] * FU).astype(jnp.int32)
    starts_out = (frag_index[MOD1:] * FU).astype(jnp.int32)

    def one_path(index):
        row_mod = index // MOD2
        col_mod = index % MOD2
        start_in = starts_in[row_mod]
        start_out = starts_out[col_mod]
        inputs = tokens[row_mod, col_mod]
        cot_rows = cotangent[row_mod, col_mod]
        up_proj = w_in[row_mod]
        down_proj = w_out[col_mod]
        stream, normed = normalize(inputs)
        preact = jnp.dot(normed, up_proj, preferred_element_type=jnp.float32)
        value, slope = gelu_parts(preact)
        hidden = value.astype(jnp.bfloat16)
        mixed = (stream + jnp.dot(hidden, down_proj, preferred_element_type=jnp.float32)).astype(jnp.bfloat16)
        down_frag = lax.dynamic_slice_in_dim(down_proj, start_in, FU, 0)
        hid_grad = jnp.dot(cot_rows, down_frag.T, preferred_element_type=jnp.float32)
        pre_grad = (hid_grad * lax.dynamic_slice_in_dim(slope, start_in, FU, 1)).astype(jnp.bfloat16)
        grad_in = jnp.dot(normed.T, pre_grad, preferred_element_type=jnp.float32)
        hid_frag = lax.dynamic_slice_in_dim(hidden, start_out, FU, 1)
        grad_out = jnp.dot(hid_frag.T, cot_rows, preferred_element_type=jnp.float32)
        return (mixed, grad_in, grad_out)
    mixed_all, grads_in, grads_out = lax.map(one_path, jnp.arange(MOD1 * MOD2, dtype=jnp.int32))
    mixed = mixed_all.reshape(MOD1, MOD2, TOK_PATH, D)
    delta_in = INNER_LR * lax.optimization_barrier(jnp.sum(grads_in.reshape(MOD1, MOD2, D, FU), axis=1))
    delta_out = INNER_LR * lax.optimization_barrier(jnp.sum(grads_out.reshape(MOD1, MOD2, FU, D), axis=0))
    new_mom_in = MOMENTUM * mom_in + delta_in
    new_mom_out = MOMENTUM * mom_out + delta_out
    in_frag = jax.vmap(lambda weight, start: lax.dynamic_slice_in_dim(weight, start, FU, 1))(w_in, starts_in).astype(jnp.float32)
    out_frag = jax.vmap(lambda weight, start: lax.dynamic_slice_in_dim(weight, start, FU, 0))(w_out, starts_out).astype(jnp.float32)
    new_in = (in_frag - OUTER_LR * (delta_in + MOMENTUM * new_mom_in)).astype(jnp.bfloat16)
    new_out = (out_frag - OUTER_LR * (delta_out + MOMENTUM * new_mom_out)).astype(jnp.bfloat16)
    return (mixed, new_in, new_mom_in, new_out, new_mom_out)
```

```python
import jax
import jax.numpy as jnp
from jax import lax
from jax.experimental import pallas as pl
from jax.experimental.pallas import tpu as pltpu
from jax.sharding import PartitionSpec as P

MESH = pl.DeviceIdType.MESH
BF, F32 = jnp.bfloat16, jnp.float32
FU = 1024
EPS = 1e-06
INNER_LR = 0.05
MOMENTUM = 0.9
OUTER_LR = 0.7
GELU_SCALE = 0.7978845608028654
GELU_CUBIC = 0.044715
DOUBLE = (False, False, True, True)


class Place:
    def __init__(p):
        p.r, p.c, p.s = lax.axis_index("row"), lax.axis_index("col"), lax.axis_index("shard")
        p.x, p.k, p.y, p.l = p.r // 2, p.r % 2, p.c // 2, p.c % 2
        p.turn = 2 * p.l - 1

    def near(p):
        return (p.r, p.y * 2 + 1 - p.l, (p.s + p.turn + 4) % 4)

    def twin(p):
        return (p.r, p.y * 2 + 1 - p.l, p.s)

    def at_y(p, d):
        return (p.r, ((p.y + d + 4) % 4) * 2 + p.l, p.s)

    def twin_y(p, d):
        return (p.r, ((p.y + d + 4) % 4) * 2 + 1 - p.l, p.s)

    def at_x(p, d):
        return (((p.x + d + 4) % 4) * 2 + p.k, p.c, p.s)

    def at_s(p, d):
        return (p.r, p.c, (p.s + d + 4) % 4)

    def twin_s(p, d):
        return (p.r, p.y * 2 + 1 - p.l, (p.s + d + 4) % 4)

    def sib(p):
        return (p.x * 2 + 1 - p.k, p.c, p.s)

    def partners(p):
        some = [p.twin(), p.sib()]
        some += [p.at_y(d) for d in (1, 2, 3)] + [p.at_x(d) for d in (1, 2, 3)] + [p.at_s(d) for d in (1, 2, 3)]
        some += [p.twin_s(d) for d in (1, 2, 3)]
        return some


class Copies:
    def __init__(self, send, recv):
        self.send, self.recv, self.sent, self.ids = send, recv, [], {}

    def at(self, name):
        return self.recv.at[self.ids.setdefault(name, len(self.ids))]

    def put(self, name, src, dst, dev):
        copy = pltpu.make_async_remote_copy(
            src_ref=src, dst_ref=dst, send_sem=self.send.at[len(self.sent)], recv_sem=self.at(name),
            device_id=dev, device_id_type=MESH,
        )
        copy.start()
        self.sent.append(copy)
        return copy

    def got(self, name, slot):
        pltpu.make_async_remote_copy(
            src_ref=slot, dst_ref=slot, send_sem=self.send.at[0], recv_sem=self.at(name),
            device_id=self.sent[0].device_id, device_id_type=MESH,
        ).wait_recv()

    def flush(self):
        for copy in self.sent:
            copy.wait_send()


def gelu(v):
    tangent = jnp.tanh(GELU_SCALE * (v + GELU_CUBIC * v * v * v))
    return tangent, 0.5 * v * (1.0 + tangent)


def slope_of(v, tangent):
    return 0.5 * (1.0 + tangent) + 0.5 * v * (1.0 - tangent * tangent) * GELU_SCALE * (
        1.0 + 3.0 * GELU_CUBIC * v * v
    )


def rows(start, size):
    return pl.ds(pl.multiple_of(start, size), size)


def kernel(
    frag, tok_hbm, cot_hbm, win_hbm, wout_hbm,
    mix_hbm, fin_hbm, fout_hbm,
    OWN, WIN, WOUT, TOK, COT, NORM, NT, HID, SLOPE, PG, GIF, GIB, RA, RB, RBR, FIN,
    GO, GOR, HT, GXF, GXB, RX, RSB, RSR, FOUT, MIX, WFRAG, HFRAG, HIDN,
    send, recv, local,
):
    p = Place()
    C = Copies(send, recv)
    y, s, r, x, k, l = p.y, p.s, p.r, p.x, p.k, p.l
    yp, ym, yf = (y + 1) % 4, (y + 3) % 4, (y + 2) % 4
    ci = frag[r]
    ej = frag[8 + p.c]
    te = lax.rem(ej - ci + 4, 4)
    quarter = [lax.rem(ci + t, 4) for t in range(4)]
    turned = [lax.rem(q - ci + 4, 4) for q in range(4)]

    fetch = []

    def load(src, dst):
        copy = pltpu.make_async_copy(src, dst, local.at[len(fetch)])
        copy.start()
        fetch.append(copy)
        return copy

    own_in = [load(win_hbm.at[0, :, pl.ds(q * 1024, 1024)], OWN.at[q]) for q in range(4)]
    tok_in = load(tok_hbm.at[0, 0], TOK)
    cot_in = load(cot_hbm.at[0, 0], COT)
    wout_in = [load(wout_hbm.at[0, pl.ds(q * 1024, 1024), :], WOUT.at[s, q]) for q in range(4)]

    barrier = pltpu.get_barrier_semaphore()
    partners = p.partners()
    for dev in partners:
        pl.semaphore_signal(barrier, inc=1, device_id=dev, device_id_type=MESH)
    pl.semaphore_wait(barrier, len(partners))

    near, twin, sib = p.near(), p.twin(), p.sib()
    shard = {"n": (s + p.turn + 4) % 4, "t": (s - p.turn + 4) % 4, "f": (s + 2) % 4}
    so = {"m": (s + 3) % 4, "p": (s + 1) % 4, "f": (s + 2) % 4}
    ox = {"0": r, "m": ((x + 3) % 4) * 2 + k, "p": ((x + 1) % 4) * 2 + k, "f": ((x + 2) % 4) * 2 + k}

    def wo(f, o, g=None):
        if g is None:
            return WOUT.at[f, o // 2, rows((o % 2) * 512, 512), :]
        return WOUT.at[f, o // 2, rows((o % 2) * 512 + g * 256, 256), :]

    mine = wout_hbm.at[0, rows(r * 512, 512), :]
    C.put("s1m", mine, wo(s, r), p.at_s(1))
    C.put("s1p", mine, wo(s, r), p.at_s(-1))

    def s_hop(side):
        if side == "m":
            C.got("s1m", wo(so["m"], r))
            C.put("s2m", wo(so["m"], r, 0), wo(so["m"], r, 0), p.at_s(1))
        else:
            C.got("s1p", wo(so["p"], r))
            C.put("s2p", wo(so["p"], r, 1), wo(so["p"], r, 1), p.at_s(-1))
        x_send(side)

    def s_last():
        C.got("s2m", wo(so["f"], r, 0))
        C.got("s2p", wo(so["f"], r, 1))
        x_send("f")

    def x_send(f):
        ref = wo(so[f], r)
        C.put(f"xm{f}", ref, ref, p.at_x(1))
        C.put(f"xp{f}", ref, ref, p.at_x(-1))
        C.put(f"c0{f}", ref, ref, sib)

    def x_hop(f):
        a, b = wo(so[f], ox["m"]), wo(so[f], ox["p"])
        C.got(f"xm{f}", a)
        ref = wo(so[f], ox["m"], 0)
        C.put(f"vm{f}", ref, ref, p.at_x(1))
        C.got(f"xp{f}", b)
        ref = wo(so[f], ox["p"], 1)
        C.put(f"vp{f}", ref, ref, p.at_x(-1))
        C.put(f"cm{f}", a, a, sib)
        C.put(f"cp{f}", b, b, sib)

    def x_last(f):
        C.got(f"vm{f}", wo(so[f], ox["f"], 0))
        C.got(f"vp{f}", wo(so[f], ox["f"], 1))
        ref = wo(so[f], ox["f"])
        C.put(f"cf{f}", ref, ref, sib)

    def core_last():
        for f in "mpf":
            for o, at in ox.items():
                C.got(f"c{o}{f}", wo(so[f], at + 1 - 2 * k))

    first, second = l, 1 - l

    def zc(t, f, h):
        if DOUBLE[t]:
            return WIN.at[t, y % 2 + 2 * h, rows(f * 256, 256), :]
        return WIN.at[t, y, rows(f * 256 + h * 128, 128), :]

    def z_start(t):
        ref = zc(t, s, first)
        C.put(f"z{t}nB", ref, ref, near)
        ref = zc(t, s, second)
        C.put(f"z{t}nA", ref, ref, near)

    def z_hop1(t):
        ref = zc(t, shard["n"], first)
        C.got(f"z{t}nA", ref)
        C.put(f"z{t}tB", ref, ref, twin)
        ref = zc(t, shard["n"], second)
        C.got(f"z{t}nB", ref)
        C.put(f"z{t}tA", ref, ref, twin)
        y_send(t, "n")

    def z_hop2(t):
        ref = zc(t, shard["t"], second)
        C.got(f"z{t}tB", ref)
        C.put(f"z{t}fA", ref, ref, near)
        C.got(f"z{t}tA", zc(t, shard["t"], first))
        y_send(t, "t")

    def z_hop3(t):
        ref = zc(t, shard["f"], first)
        C.got(f"z{t}fA", ref)
        C.put(f"z{t}fB", ref, ref, twin)

    def z_hop4(t):
        C.got(f"z{t}fB", zc(t, shard["f"], second))
        y_send(t, "f")

    def blk(t, u, f, h=None):
        if h is None:
            return WIN.at[t, u, rows(shard[f] * 256, 256), :]
        return WIN.at[t, u, rows(shard[f] * 256 + h * 128, 128), :]

    def from_m(t):
        return (y + 1) % 2 if DOUBLE[t] else ym

    def from_p(t):
        return (y + 1) % 2 + 2 if DOUBLE[t] else yp

    def y_send(t, f):
        a = blk(t, y % 2 if DOUBLE[t] else y, f)
        b = blk(t, y % 2 + 2 if DOUBLE[t] else y, f)
        C.put(f"y{t}{f}m", a, a, p.at_y(1))
        C.put(f"y{t}{f}p", b, b, p.at_y(-1))

    def y_hop(t, f):
        C.got(f"y{t}{f}m", blk(t, from_m(t), f))
        if not DOUBLE[t]:
            ref = blk(t, ym, f, 0)
            C.put(f"w{t}{f}m", ref, ref, p.at_y(1))
        C.got(f"y{t}{f}p", blk(t, from_p(t), f))
        if not DOUBLE[t]:
            ref = blk(t, yp, f, 1)
            C.put(f"w{t}{f}p", ref, ref, p.at_y(-1))

    def y_last(t):
        if not DOUBLE[t]:
            for f in "ntf":
                C.got(f"w{t}{f}m", blk(t, yf, f, 0))
                C.got(f"w{t}{f}p", blk(t, yf, f, 1))

    def place_own(t):
        block = OWN[quarter[t]]
        for u in range(4):
            WIN[t, u, rows(s * 256, 256), :] = block[:, u * 256 : u * 256 + 256]

    def normalize():
        @pl.loop(0, 8)
        def _(i):
            at = rows(i * 64, 64)
            stream = TOK[at, :].astype(F32)
            mean = jnp.mean(stream * stream, axis=-1, keepdims=True)
            NORM[at, :] = (stream * lax.rsqrt(mean + EPS)).astype(BF)

    def transpose_normed():
        for i in range(4):
            NT[:, i * 128 : i * 128 + 128] = NORM[i * 128 : i * 128 + 128, :].T

    def up(t, u):
        @pl.loop(0, 2)
        def _(i):
            at = rows(i * 256, 256)
            v = jnp.dot(NORM[at, :], WIN[t, u], preferred_element_type=F32)
            tangent, value = gelu(v)
            HID[t, at, rows(u * 256, 256)] = value.astype(BF)
            if t == 0:
                SLOPE[u, at, :] = slope_of(v, tangent)

    def up_all(t):
        for u in (y, ym, yp, yf):
            up(t, u)

    def take_fragment():
        for b in range(4):
            WFRAG[b] = WOUT[b, ci]

    def pre_grad(u):
        @pl.loop(0, 2)
        def _(i):
            at = rows(i * 256, 256)
            total = jnp.zeros((256, 256), F32)
            for b in range(4):
                total += lax.dot_general(
                    COT[at, b * 256 : b * 256 + 256],
                    WFRAG[b, rows(u * 256, 256), :],
                    (((1,), (1,)), ((), ())),
                    preferred_element_type=F32,
                )
            PG[u, at, :] = (total * SLOPE[u, at, :]).astype(BF)

    def grad_in(u, out):
        @pl.loop(0, 4)
        def _(i):
            at = rows(i * 256, 256)
            out[at, :] = jnp.dot(NT[at, :], PG[u], preferred_element_type=F32).astype(out.dtype)

    LO, HI = pl.ds(0, 512), pl.ds(512, 512)

    def in_start():
        pre_grad(yf)
        grad_in(yf, GIB.at[2])
        C.put("ai0", GIB.at[2, LO], RA.at[0], p.at_y(1))
        C.put("ai1", GIB.at[2, HI], RA.at[1], p.at_y(-1))
        pre_grad(yp)
        grad_in(yp, GIB.at[0])
        C.put("ai2", GIB.at[0, HI], RA.at[2], p.at_y(1))
        pre_grad(ym)
        grad_in(ym, GIB.at[1])
        C.put("ai3", GIB.at[1, LO], RA.at[3], p.at_y(-1))

    def in_relay():
        C.got("ai0", RA.at[0])
        GIB[0, LO, :] = (GIB[0, LO, :].astype(F32) + RA[0].astype(F32)).astype(BF)
        C.put("ai4", GIB.at[0, LO], RA.at[4], p.at_y(1))
        C.got("ai1", RA.at[1])
        GIB[1, HI, :] = (GIB[1, HI, :].astype(F32) + RA[1].astype(F32)).astype(BF)
        C.put("ai5", GIB.at[1, HI], RA.at[5], p.at_y(-1))
        pre_grad(y)
        grad_in(y, GIF)

    zs = [(d, e) for d in range(4) for e in range(2) if (d, e) != (0, 0)]

    def in_sum():
        C.got("ai2", RA.at[2])
        C.got("ai3", RA.at[3])
        C.got("ai4", RA.at[4])
        C.got("ai5", RA.at[5])
        RB[LO, :] = (GIF[LO, :] + RA[3].astype(F32) + RA[4].astype(F32)).astype(BF)
        RB[HI, :] = (GIF[HI, :] + RA[2].astype(F32) + RA[5].astype(F32)).astype(BF)
        for n, (d, e) in enumerate(zs):
            piece = rows(((s + d) % 4) * 256 + (l + e - 2 * l * e) * 128, 128)
            dev = p.at_s(d) if e == 0 else p.twin_s(d)
            C.put(f"bi{n}", RB.at[piece], RBR.at[n], dev)

    def in_result():
        total = RB[rows(s * 256 + l * 128, 128), :].astype(F32)
        for n in range(7):
            C.got(f"bi{n}", RBR.at[n])
            total += RBR[n].astype(F32)
        FIN[y, l] = total.astype(BF)
        ref = FIN.at[y, l]
        C.put("ct", ref, ref, twin)
        C.put("cm0", ref, ref, p.at_y(1))
        C.put("cp0", ref, ref, p.at_y(-1))

    def in_spread():
        other = FIN.at[y, 1 - l]
        C.got("ct", other)
        C.put("cm1", other, other, p.at_y(1))
        C.put("cp1", other, other, p.at_y(-1))
        C.got("cm0", FIN.at[ym, l])
        ref = FIN.at[ym, l]
        C.put("cf0", ref, ref, p.at_y(1))
        C.got("cp0", FIN.at[yp, l])
        C.got("cp1", FIN.at[yp, 1 - l])
        ref = FIN.at[yp, 1 - l]
        C.put("cf1", ref, ref, p.at_y(-1))
        C.got("cm1", FIN.at[ym, 1 - l])
        C.got("cf0", FIN.at[yf, l])
        C.got("cf1", FIN.at[yf, 1 - l])

    def grad_out(half, out):
        for v in range(2):
            u = half * 2 + v
            HT[...] = HFRAG[:, rows(u * 256, 256)].T

            @pl.loop(0, 4)
            def _(i):
                at = rows(i * 256, 256)
                out[v, :, at] = jnp.dot(HT[...], COT[:, at], preferred_element_type=F32)

    def in_place():
        for q in range(4):
            HIDN[q] = HID[turned[q]]

    def out_start():
        HFRAG[...] = HID[te]
        grad_out(1 - k, GO.at[1])
        C.put("g0", GO.at[1], GOR, sib)
        grad_out(k, GO.at[0])

    def part(d):
        o = (x + d) % 4
        return o // 2, rows((o % 2) * 128, 128)

    def out_reduce():
        C.got("g0", GOR)
        for slot, d in ((2, 2), (0, 1), (1, 3), (None, 0)):
            b, at = part(d)
            total = GO[0, b, at, :] + GOR[b, at, :]
            if slot is None:
                GXF[...] = total
            else:
                GXB[slot] = total.astype(BF)
            if slot == 2:
                C.put("gx0", GXB.at[2, pl.ds(0, 64)], RX.at[0], p.at_x(1))
                C.put("gx1", GXB.at[2, pl.ds(64, 64)], RX.at[1], p.at_x(-1))
            if slot == 0:
                C.put("gx2", GXB.at[0, pl.ds(64, 64)], RX.at[2], p.at_x(1))
            if slot == 1:
                C.put("gx3", GXB.at[1, pl.ds(0, 64)], RX.at[3], p.at_x(-1))

    def out_relay():
        C.got("gx0", RX.at[0])
        GXB[0, 0:64, :] = (GXB[0, 0:64, :].astype(F32) + RX[0].astype(F32)).astype(BF)
        C.put("gx4", GXB.at[0, pl.ds(0, 64)], RX.at[4], p.at_x(1))
        C.got("gx1", RX.at[1])
        GXB[1, 64:128, :] = (GXB[1, 64:128, :].astype(F32) + RX[1].astype(F32)).astype(BF)
        C.put("gx5", GXB.at[1, pl.ds(64, 64)], RX.at[5], p.at_x(-1))

    def out_sum():
        for n in (2, 3, 4, 5):
            C.got(f"gx{n}", RX.at[n])
        for b in range(4):
            at = pl.ds(b * 256, 256)
            RSB[b, 0:64, :] = (GXF[0:64, at] + RX[3, :, at].astype(F32) + RX[4, :, at].astype(F32)).astype(BF)
            RSB[b, 64:128, :] = (GXF[64:128, at] + RX[2, :, at].astype(F32) + RX[5, :, at].astype(F32)).astype(BF)
        for d in (2, 1, 3):
            C.put(f"gs{d}", RSB.at[(s + d) % 4], RSR.at[d - 1], p.at_s(d))

    def out_result():
        total = RSB[s].astype(F32)
        for d in (1, 2, 3):
            C.got(f"gs{d}", RSR.at[d - 1])
            total += RSR[d - 1].astype(F32)
        FOUT[k, x] = total.astype(BF)
        ref = FOUT.at[k, x]
        C.put("hm", ref, ref, p.at_x(1))
        C.put("hp", ref, ref, p.at_x(-1))
        C.put("hf", ref, ref, p.at_x(2))
        C.put("h0", ref, ref, sib)

    def out_spread():
        for n, d in (("m", 3), ("p", 1), ("f", 2)):
            ref = FOUT.at[k, (x + d) % 4]
            C.got("h" + n, ref)
            C.put("i" + n, ref, ref, sib)
        for n, d in (("h0", 0), ("im", 3), ("ip", 1), ("if", 2)):
            C.got(n, FOUT.at[1 - k, (x + d) % 4])

    def down(b):
        @pl.loop(0, 2)
        def _(i):
            at = rows(i * 256, 256)
            total = TOK[at, b * 256 : b * 256 + 256].astype(F32)
            for t in range(4):
                total += jnp.dot(
                    HIDN[t, at, :], WOUT[b, t], preferred_element_type=F32
                )
            MIX[at, b * 256 : b * 256 + 256] = total.astype(BF)

    for copy in own_in:
        copy.wait()
    place_own(0)
    z_start(0)
    for t in (1, 2, 3):
        place_own(t)
    tok_in.wait()
    normalize()
    z_hop1(0)
    s_hop("m")
    s_hop("p")
    z_hop2(0)
    z_start(1)
    transpose_normed()
    x_hop("m")
    z_hop3(0)
    z_hop4(0)
    z_hop1(1)
    s_last()
    y_hop(0, "n")
    y_hop(0, "t")
    x_hop("p")
    z_hop2(1)
    z_start(2)
    y_hop(0, "f")
    x_last("m")
    z_hop3(1)
    z_hop4(1)
    x_hop("f")
    x_last("p")
    z_hop1(2)
    y_last(0)
    y_hop(1, "n")
    y_hop(1, "t")
    up(0, y)
    up(0, ym)
    x_last("f")
    z_hop2(2)
    z_start(3)
    up(0, yp)
    up(0, yf)
    y_hop(1, "f")
    z_hop3(2)
    z_hop4(2)
    cot_in.wait()
    for copy in wout_in:
        copy.wait()
    core_last()
    take_fragment()
    in_start()
    z_hop1(3)
    y_last(1)
    up(1, y)
    up(1, ym)
    z_hop2(3)
    up(1, yp)
    up(1, yf)
    in_relay()
    for f in "ntf":
        y_hop(2, f)
    z_hop3(3)
    z_hop4(3)
    up_all(2)
    for f in "ntf":
        y_hop(3, f)
    up_all(3)
    out_start()
    in_sum()
    in_place()
    out_reduce()
    down(0)
    out_relay()
    down(1)
    out_sum()
    in_result()
    down(2)
    out_result()
    in_spread()
    down(3)
    out_spread()

    stores = []
    for n, (src, dst) in enumerate(((MIX, mix_hbm.at[0, 0]), (FIN, fin_hbm), (FOUT, fout_hbm))):
        copy = pltpu.make_async_copy(src, dst, local.at[len(fetch) + n])
        copy.start()
        stores.append(copy)
    C.flush()
    for copy in stores:
        copy.wait()


SCRATCH = [
    ((4, 256, 1024), BF),
    ((4, 4, 1024, 256), BF),
    ((4, 4, 1024, 256), BF),
    ((512, 1024), BF),
    ((512, 1024), BF),
    ((512, 1024), BF),
    ((1024, 512), BF),
    ((4, 512, 1024), BF),
    ((4, 512, 256), F32),
    ((4, 512, 256), BF),
    ((1024, 256), F32),
    ((3, 1024, 256), BF),
    ((6, 512, 256), BF),
    ((1024, 256), BF),
    ((7, 128, 256), BF),
    ((4, 2, 128, 256), BF),
    ((2, 2, 256, 1024), F32),
    ((2, 256, 1024), F32),
    ((256, 512), BF),
    ((128, 1024), F32),
    ((3, 128, 1024), BF),
    ((6, 64, 1024), BF),
    ((4, 128, 256), BF),
    ((3, 128, 256), BF),
    ((2, 4, 128, 256), BF),
    ((512, 1024), BF),
    ((4, 1024, 256), BF),
    ((512, 1024), BF),
    ((4, 512, 1024), BF),
]


def path_step(frag_index, tokens, cotangent, w_in, w_out):
    anywhere = pl.BlockSpec(memory_space=pl.ANY)
    return pl.pallas_call(
        kernel,
        out_shape=(
            jax.ShapeDtypeStruct((1, 1, 512, 1024), BF),
            jax.ShapeDtypeStruct((4, 2, 128, 256), BF),
            jax.ShapeDtypeStruct((2, 4, 128, 256), BF),
        ),
        in_specs=[pl.BlockSpec(memory_space=pltpu.SMEM)] + [anywhere] * 4,
        out_specs=(anywhere,) * 3,
        scratch_shapes=[pltpu.VMEM(shape, dtype) for shape, dtype in SCRATCH]
        + [pltpu.SemaphoreType.DMA((180,)), pltpu.SemaphoreType.DMA((180,)), pltpu.SemaphoreType.DMA((16,))],
        compiler_params=pltpu.CompilerParams(
            collective_id=0, has_side_effects=True, vmem_limit_bytes=60 * 2**20
        ),
        cost_estimate=pl.CostEstimate(flops=12 * 2**30, bytes_accessed=24 * 2**20, transcendentals=2**21),
        name="path_step",
    )(frag_index, tokens, cotangent, w_in, w_out)


def shards(tokens, cotangent, w_in, w_out, frag_index, mom_in, mom_out):
    start_in = frag_index[lax.axis_index("row")] * FU
    start_out = frag_index[lax.axis_size("row") + lax.axis_index("col")] * FU
    mixed, sums_in, sums_out = path_step(frag_index, tokens, cotangent, w_in, w_out)
    summed_in = sums_in.transpose(1, 2, 0, 3).reshape(256, FU).astype(F32)
    summed_out = sums_out.reshape(FU, 256).astype(F32)
    delta_in = INNER_LR * summed_in
    delta_out = INNER_LR * summed_out
    new_mom_in = MOMENTUM * mom_in[0] + delta_in
    new_mom_out = MOMENTUM * mom_out[0] + delta_out
    in_frag = lax.dynamic_slice_in_dim(w_in[0], start_in, FU, 1).astype(F32)
    out_frag = lax.dynamic_slice_in_dim(w_out[0], start_out, FU, 0).astype(F32)
    new_in = (in_frag - OUTER_LR * (delta_in + MOMENTUM * new_mom_in)).astype(BF)
    new_out = (out_frag - OUTER_LR * (delta_out + MOMENTUM * new_mom_out)).astype(BF)
    return (mixed, new_in[None], new_mom_in[None], new_out[None], new_mom_out[None])


def solution(mesh):
    placed = (
        P("row", "col", "shard", None),
        P("row", "col", "shard", None),
        P("row", "shard", None),
        P("col", None, "shard"),
        P(),
        P("row", "shard", None),
        P("col", None, "shard"),
    )
    return jax.shard_map(
        shards,
        mesh=mesh,
        in_specs=placed,
        out_specs=(
            P("row", "col", "shard", None),
            P("row", "shard", None),
            P("row", "shard", None),
            P("col", None, "shard"),
            P("col", None, "shard"),
        ),
        check_vma=False,
    )
```

```python
import jax
import jax.numpy as jnp
from jax import lax
from jax.experimental import pallas as pl
from jax.experimental.pallas import tpu as pltpu
from jax.sharding import PartitionSpec as P

MESH = pl.DeviceIdType.MESH
BF, F32 = jnp.bfloat16, jnp.float32
FU = 1024
EPS = 1e-06
INNER_LR = 0.05
MOMENTUM = 0.9
OUTER_LR = 0.7
GELU_SCALE = 0.7978845608028654
GELU_CUBIC = 0.044715
DOUBLE = (False, False, True, True)


class Place:
    def __init__(p):
        p.r, p.c, p.s = lax.axis_index("row"), lax.axis_index("col"), lax.axis_index("shard")
        p.x, p.k, p.y, p.l = p.r // 2, p.r % 2, p.c // 2, p.c % 2
        p.turn = 2 * p.l - 1

    def near(p):
        return (p.r, p.y * 2 + 1 - p.l, (p.s + p.turn + 4) % 4)

    def twin(p):
        return (p.r, p.y * 2 + 1 - p.l, p.s)

    def at_y(p, d):
        return (p.r, ((p.y + d + 4) % 4) * 2 + p.l, p.s)

    def twin_y(p, d):
        return (p.r, ((p.y + d + 4) % 4) * 2 + 1 - p.l, p.s)

    def at_x(p, d):
        return (((p.x + d + 4) % 4) * 2 + p.k, p.c, p.s)

    def at_s(p, d):
        return (p.r, p.c, (p.s + d + 4) % 4)

    def twin_s(p, d):
        return (p.r, p.y * 2 + 1 - p.l, (p.s + d + 4) % 4)

    def sib(p):
        return (p.x * 2 + 1 - p.k, p.c, p.s)

    def partners(p):
        some = [p.twin(), p.sib()]
        some += [p.at_y(d) for d in (1, 2, 3)] + [p.at_x(d) for d in (1, 2, 3)] + [p.at_s(d) for d in (1, 2, 3)]
        some += [p.twin_s(d) for d in (1, 2, 3)]
        return some


class Copies:
    def __init__(self, send, recv):
        self.send, self.recv, self.sent, self.ids = send, recv, [], {}

    def at(self, name):
        return self.recv.at[self.ids.setdefault(name, len(self.ids))]

    def put(self, name, src, dst, dev):
        copy = pltpu.make_async_remote_copy(
            src_ref=src, dst_ref=dst, send_sem=self.send.at[len(self.sent)], recv_sem=self.at(name),
            device_id=dev, device_id_type=MESH,
        )
        copy.start()
        self.sent.append(copy)
        return copy

    def got(self, name, slot):
        pltpu.make_async_remote_copy(
            src_ref=slot, dst_ref=slot, send_sem=self.send.at[0], recv_sem=self.at(name),
            device_id=self.sent[0].device_id, device_id_type=MESH,
        ).wait_recv()

    def flush(self):
        for copy in self.sent:
            copy.wait_send()


def gelu(v):
    tangent = jnp.tanh(GELU_SCALE * (v + GELU_CUBIC * v * v * v))
    return tangent, 0.5 * v * (1.0 + tangent)


def slope_of(v, tangent):
    return 0.5 * (1.0 + tangent) + 0.5 * v * (1.0 - tangent * tangent) * GELU_SCALE * (
        1.0 + 3.0 * GELU_CUBIC * v * v
    )


def rows(start, size):
    return pl.ds(pl.multiple_of(start, size), size)


def kernel(
    frag, tok_hbm, cot_hbm, win_hbm, wout_hbm,
    mix_hbm, fin_hbm, fout_hbm,
    OWN, WIN, WOUT, TOK, COT, NORM, NT, HID, SLOPE, PG, GIF, GIB, RA, RB, RBR, FIN,
    GO, GOR, HT, GXF, GXB, RX, RSB, RSR, FOUT, MIX, WFRAG, HFRAG, HIDN,
    send, recv, local,
):
    p = Place()
    C = Copies(send, recv)
    y, s, r, x, k, l = p.y, p.s, p.r, p.x, p.k, p.l
    yp, ym, yf = (y + 1) % 4, (y + 3) % 4, (y + 2) % 4
    ci = frag[r]
    ej = frag[8 + p.c]
    te = lax.rem(ej - ci + 4, 4)
    quarter = [lax.rem(ci + t, 4) for t in range(4)]
    turned = [lax.rem(q - ci + 4, 4) for q in range(4)]

    fetch, mix_out = [], []

    def load(src, dst):
        copy = pltpu.make_async_copy(src, dst, local.at[len(fetch)])
        copy.start()
        fetch.append(copy)
        return copy

    own_in = [load(win_hbm.at[0, :, pl.ds(q * 1024, 1024)], OWN.at[q]) for q in range(4)]
    tok_in = load(tok_hbm.at[0, 0], TOK)
    cot_in = load(cot_hbm.at[0, 0], COT)
    wout_in = [load(wout_hbm.at[0, pl.ds(q * 1024, 1024), :], WOUT.at[s, q]) for q in range(4)]

    barrier = pltpu.get_barrier_semaphore()
    partners = p.partners()
    for dev in partners:
        pl.semaphore_signal(barrier, inc=1, device_id=dev, device_id_type=MESH)
    pl.semaphore_wait(barrier, len(partners))

    near, twin, sib = p.near(), p.twin(), p.sib()
    shard = {"n": (s + p.turn + 4) % 4, "t": (s - p.turn + 4) % 4, "f": (s + 2) % 4}
    so = {"m": (s + 3) % 4, "p": (s + 1) % 4, "f": (s + 2) % 4}
    ox = {"0": r, "m": ((x + 3) % 4) * 2 + k, "p": ((x + 1) % 4) * 2 + k, "f": ((x + 2) % 4) * 2 + k}

    def wo(f, o, g=None):
        if g is None:
            return WOUT.at[f, o // 2, rows((o % 2) * 512, 512), :]
        return WOUT.at[f, o // 2, rows((o % 2) * 512 + g * 256, 256), :]

    def s_start():
        mine = wout_hbm.at[0, rows(r * 512, 512), :]
        C.put("s1m", mine, wo(s, r), p.at_s(1))
        C.put("s1p", mine, wo(s, r), p.at_s(-1))

    def s_hop(side):
        if side == "m":
            C.got("s1m", wo(so["m"], r))
            ref = wo(so["m"], r, 0)
            C.put("s2m", ref, ref, p.at_s(1))
        else:
            C.got("s1p", wo(so["p"], r))
            ref = wo(so["p"], r, 1)
            C.put("s2p", ref, ref, p.at_s(-1))

    def s_last():
        C.got("s2m", wo(so["f"], r, 0))
        C.got("s2p", wo(so["f"], r, 1))

    def x_send(f):
        ref = wo(so[f], r)
        C.put(f"xm{f}", ref, ref, p.at_x(1))
        C.put(f"xp{f}", ref, ref, p.at_x(-1))
        C.put(f"c0{f}", ref, ref, sib)

    def x_hop(f):
        a, b = wo(so[f], ox["m"]), wo(so[f], ox["p"])
        C.got(f"xm{f}", a)
        ref = wo(so[f], ox["m"], 0)
        C.put(f"vm{f}", ref, ref, p.at_x(1))
        C.got(f"xp{f}", b)
        ref = wo(so[f], ox["p"], 1)
        C.put(f"vp{f}", ref, ref, p.at_x(-1))
        C.put(f"cm{f}", a, a, sib)
        C.put(f"cp{f}", b, b, sib)

    def x_last(f):
        C.got(f"vm{f}", wo(so[f], ox["f"], 0))
        C.got(f"vp{f}", wo(so[f], ox["f"], 1))
        ref = wo(so[f], ox["f"])
        C.put(f"cf{f}", ref, ref, sib)

    def core_last():
        for copy in wout_in:
            copy.wait()
        for f in "mpf":
            for o, at in ox.items():
                C.got(f"c{o}{f}", wo(so[f], at + 1 - 2 * k))

    first, second = l, 1 - l

    def zc(t, f, h):
        if DOUBLE[t]:
            return WIN.at[t, y % 2 + 2 * h, rows(f * 256, 256), :]
        return WIN.at[t, y, rows(f * 256 + h * 128, 128), :]

    def z_start(t):
        ref = zc(t, s, first)
        C.put(f"z{t}nB", ref, ref, near)
        ref = zc(t, s, second)
        C.put(f"z{t}nA", ref, ref, near)

    def z_hop1(t):
        ref = zc(t, shard["n"], first)
        C.got(f"z{t}nA", ref)
        C.put(f"z{t}tB", ref, ref, twin)
        ref = zc(t, shard["n"], second)
        C.got(f"z{t}nB", ref)
        C.put(f"z{t}tA", ref, ref, twin)
        y_send(t, "n")

    def z_hop2(t):
        ref = zc(t, shard["t"], second)
        C.got(f"z{t}tB", ref)
        C.put(f"z{t}fA", ref, ref, near)
        C.got(f"z{t}tA", zc(t, shard["t"], first))
        y_send(t, "t")

    def z_hop3(t):
        ref = zc(t, shard["f"], first)
        C.got(f"z{t}fA", ref)
        C.put(f"z{t}fB", ref, ref, twin)

    def z_hop4(t):
        C.got(f"z{t}fB", zc(t, shard["f"], second))
        y_send(t, "f")

    def blk(t, u, f, h=None):
        if h is None:
            return WIN.at[t, u, rows(shard[f] * 256, 256), :]
        return WIN.at[t, u, rows(shard[f] * 256 + h * 128, 128), :]

    def from_m(t):
        return (y + 1) % 2 if DOUBLE[t] else ym

    def from_p(t):
        return (y + 1) % 2 + 2 if DOUBLE[t] else yp

    def y_send(t, f):
        a = blk(t, y % 2 if DOUBLE[t] else y, f)
        b = blk(t, y % 2 + 2 if DOUBLE[t] else y, f)
        C.put(f"y{t}{f}m", a, a, p.at_y(1))
        C.put(f"y{t}{f}p", b, b, p.at_y(-1))

    def y_hop(t, f):
        C.got(f"y{t}{f}m", blk(t, from_m(t), f))
        if not DOUBLE[t]:
            ref = blk(t, ym, f, 0)
            C.put(f"w{t}{f}m", ref, ref, p.at_y(1))
        C.got(f"y{t}{f}p", blk(t, from_p(t), f))
        if not DOUBLE[t]:
            ref = blk(t, yp, f, 1)
            C.put(f"w{t}{f}p", ref, ref, p.at_y(-1))

    def y_last(t):
        if not DOUBLE[t]:
            for f in "ntf":
                C.got(f"w{t}{f}m", blk(t, yf, f, 0))
                C.got(f"w{t}{f}p", blk(t, yf, f, 1))

    def place_own(t):
        block = OWN[quarter[t]]
        for u in range(4):
            WIN[t, u, rows(s * 256, 256), :] = block[:, u * 256 : u * 256 + 256]

    def normalize():
        tok_in.wait()

        @pl.loop(0, 8)
        def _(i):
            at = rows(i * 64, 64)
            stream = TOK[at, :].astype(F32)
            mean = jnp.mean(stream * stream, axis=-1, keepdims=True)
            NORM[at, :] = (stream * lax.rsqrt(mean + EPS)).astype(BF)

    def transpose_normed():
        for i in range(4):
            NT[:, i * 128 : i * 128 + 128] = NORM[i * 128 : i * 128 + 128, :].T

    def up(t, u):
        @pl.loop(0, 2)
        def _(i):
            at = rows(i * 256, 256)
            v = jnp.dot(NORM[at, :], WIN[t, u], preferred_element_type=F32)
            tangent, value = gelu(v)
            HID[t, at, rows(u * 256, 256)] = value.astype(BF)
            if t == 0:
                SLOPE[u, at, :] = slope_of(v, tangent)

    def block_at(t, n):
        if DOUBLE[t]:
            return (y % 2, y % 2 + 2, (y + 1) % 2, (y + 1) % 2 + 2)[n]
        return (y, ym, yp, yf)[n]

    def take_fragment():
        for b in range(4):
            WFRAG[b] = WOUT[b, ci]

    def pre_grad(u):
        @pl.loop(0, 2)
        def _(i):
            at = rows(i * 256, 256)
            total = jnp.zeros((256, 256), F32)
            for b in range(4):
                total += lax.dot_general(
                    COT[at, b * 256 : b * 256 + 256],
                    WFRAG[b, rows(u * 256, 256), :],
                    (((1,), (1,)), ((), ())),
                    preferred_element_type=F32,
                )
            PG[u, at, :] = (total * SLOPE[u, at, :]).astype(BF)

    def grad_in(u, out):
        @pl.loop(0, 4)
        def _(i):
            at = rows(i * 256, 256)
            out[at, :] = jnp.dot(NT[at, :], PG[u], preferred_element_type=F32).astype(out.dtype)

    LO, HI = pl.ds(0, 512), pl.ds(512, 512)

    def in_part(n):
        u = (yf, yp, ym, y)[n]
        pre_grad(u)
        grad_in(u, (GIB.at[2], GIB.at[0], GIB.at[1], GIF)[n])
        if n == 0:
            C.put("ai0", GIB.at[2, LO], RA.at[0], p.at_y(1))
            C.put("ai1", GIB.at[2, HI], RA.at[1], p.at_y(-1))
        if n == 1:
            C.put("ai2", GIB.at[0, HI], RA.at[2], p.at_y(1))
        if n == 2:
            C.put("ai3", GIB.at[1, LO], RA.at[3], p.at_y(-1))

    def in_relay(side):
        if side == 0:
            C.got("ai0", RA.at[0])
            GIB[0, LO, :] = (GIB[0, LO, :].astype(F32) + RA[0].astype(F32)).astype(BF)
            C.put("ai4", GIB.at[0, LO], RA.at[4], p.at_y(1))
        else:
            C.got("ai1", RA.at[1])
            GIB[1, HI, :] = (GIB[1, HI, :].astype(F32) + RA[1].astype(F32)).astype(BF)
            C.put("ai5", GIB.at[1, HI], RA.at[5], p.at_y(-1))

    zs = [(d, e) for d in range(4) for e in range(2) if (d, e) != (0, 0)]

    def in_sum():
        C.got("ai2", RA.at[2])
        C.got("ai3", RA.at[3])
        C.got("ai4", RA.at[4])
        C.got("ai5", RA.at[5])
        RB[LO, :] = (GIF[LO, :] + RA[3].astype(F32) + RA[4].astype(F32)).astype(BF)
        RB[HI, :] = (GIF[HI, :] + RA[2].astype(F32) + RA[5].astype(F32)).astype(BF)
        for n, (d, e) in enumerate(zs):
            piece = rows(((s + d) % 4) * 256 + (l + e - 2 * l * e) * 128, 128)
            dev = p.at_s(d) if e == 0 else p.twin_s(d)
            C.put(f"bi{n}", RB.at[piece], RBR.at[n], dev)

    def in_result():
        total = RB[rows(s * 256 + l * 128, 128), :].astype(F32)
        for n in range(7):
            C.got(f"bi{n}", RBR.at[n])
            total += RBR[n].astype(F32)
        FIN[y, l] = total.astype(BF)
        ref = FIN.at[y, l]
        C.put("ct", ref, ref, twin)
        C.put("cm0", ref, ref, p.at_y(1))
        C.put("cp0", ref, ref, p.at_y(-1))

    def in_spread():
        other = FIN.at[y, 1 - l]
        C.got("ct", other)
        C.put("cm1", other, other, p.at_y(1))
        C.put("cp1", other, other, p.at_y(-1))

    def in_spread_more():
        C.got("cm0", FIN.at[ym, l])
        ref = FIN.at[ym, l]
        C.put("cf0", ref, ref, p.at_y(1))
        C.got("cp1", FIN.at[yp, 1 - l])
        ref = FIN.at[yp, 1 - l]
        C.put("cf1", ref, ref, p.at_y(-1))
        C.got("cp0", FIN.at[yp, l])
        C.got("cm1", FIN.at[ym, 1 - l])

    def in_last():
        C.got("cf0", FIN.at[yf, l])
        C.got("cf1", FIN.at[yf, 1 - l])

    def grad_out(half, v, out):
        HT[...] = HFRAG[:, rows((half * 2 + v) * 256, 256)].T

        @pl.loop(0, 4)
        def _(i):
            at = rows(i * 256, 256)
            out[v, :, at] = jnp.dot(HT[...], COT[:, at], preferred_element_type=F32)

    def in_place():
        for q in range(4):
            HIDN[q] = HID[turned[q]]

    def out_start(v):
        if v == 0:
            HFRAG[...] = HID[te]
        grad_out(1 - k, v, GO.at[1])
        C.put(f"g{v}", GO.at[1, v], GOR.at[v], sib)

    def out_own():
        for v in range(2):
            grad_out(k, v, GO.at[0])

    def part(d):
        o = (x + d) % 4
        return o // 2, rows((o % 2) * 128, 128)

    def out_reduce():
        C.got("g0", GOR.at[0])
        C.got("g1", GOR.at[1])
        for slot, d in ((2, 2), (0, 1), (1, 3), (None, 0)):
            b, at = part(d)
            total = GO[0, b, at, :] + GOR[b, at, :]
            if slot is None:
                GXF[...] = total
            else:
                GXB[slot] = total.astype(BF)
            if slot == 2:
                C.put("gx0", GXB.at[2, pl.ds(0, 64)], RX.at[0], p.at_x(1))
                C.put("gx1", GXB.at[2, pl.ds(64, 64)], RX.at[1], p.at_x(-1))
            if slot == 0:
                C.put("gx2", GXB.at[0, pl.ds(64, 64)], RX.at[2], p.at_x(1))
            if slot == 1:
                C.put("gx3", GXB.at[1, pl.ds(0, 64)], RX.at[3], p.at_x(-1))

    def out_relay():
        C.got("gx0", RX.at[0])
        GXB[0, 0:64, :] = (GXB[0, 0:64, :].astype(F32) + RX[0].astype(F32)).astype(BF)
        C.put("gx4", GXB.at[0, pl.ds(0, 64)], RX.at[4], p.at_x(1))
        C.got("gx1", RX.at[1])
        GXB[1, 64:128, :] = (GXB[1, 64:128, :].astype(F32) + RX[1].astype(F32)).astype(BF)
        C.put("gx5", GXB.at[1, pl.ds(64, 64)], RX.at[5], p.at_x(-1))

    def out_sum():
        for n in (2, 3, 4, 5):
            C.got(f"gx{n}", RX.at[n])
        for b in range(4):
            at = pl.ds(b * 256, 256)
            RSB[b, 0:64, :] = (GXF[0:64, at] + RX[3, :, at].astype(F32) + RX[4, :, at].astype(F32)).astype(BF)
            RSB[b, 64:128, :] = (GXF[64:128, at] + RX[2, :, at].astype(F32) + RX[5, :, at].astype(F32)).astype(BF)
        for d in (2, 1, 3):
            C.put(f"gs{d}", RSB.at[(s + d) % 4], RSR.at[d - 1], p.at_s(d))

    def out_result():
        total = RSB[s].astype(F32)
        for d in (1, 2, 3):
            C.got(f"gs{d}", RSR.at[d - 1])
            total += RSR[d - 1].astype(F32)
        FOUT[k, x] = total.astype(BF)
        ref = FOUT.at[k, x]
        C.put("hm", ref, ref, p.at_x(1))
        C.put("hp", ref, ref, p.at_x(-1))
        C.put("hf", ref, ref, p.at_x(2))
        C.put("h0", ref, ref, sib)

    def out_spread():
        for n, d in (("m", 3), ("p", 1), ("f", 2)):
            ref = FOUT.at[k, (x + d) % 4]
            C.got("h" + n, ref)
            C.put("i" + n, ref, ref, sib)

    def out_last():
        for n, d in (("h0", 0), ("im", 3), ("ip", 1), ("if", 2)):
            C.got(n, FOUT.at[1 - k, (x + d) % 4])

    def down(b):
        @pl.loop(0, 2)
        def _(i):
            at = rows(i * 256, 256)
            total = TOK[at, b * 256 : b * 256 + 256].astype(F32)
            for t in range(4):
                total += jnp.dot(
                    HIDN[t, at, :], WOUT[b, t], preferred_element_type=F32
                )
            MIX[at, b * 256 : b * 256 + 256] = total.astype(BF)

        mix_out.append(load(MIX.at[:, pl.ds(b * 256, 256)], mix_hbm.at[0, 0, :, pl.ds(b * 256, 256)]))

    s_start()
    for copy in own_in:
        copy.wait()
    place_own(0)
    z_start(0)
    place_own(1)
    z_hop1(0)
    z_start(1)
    z_hop2(0)
    place_own(2)
    z_start(2)
    z_hop1(1)
    normalize()
    z_hop3(0)
    s_hop("m")
    x_send("m")
    z_hop2(1)
    y_hop(0, "t")
    y_hop(0, "n")
    s_hop("p")
    z_hop4(0)
    x_send("p")
    place_own(3)
    transpose_normed()
    y_hop(1, "t")
    y_hop(1, "n")
    z_start(3)
    z_hop1(2)
    s_last()
    x_send("f")
    z_hop3(1)
    y_hop(0, "f")
    z_hop1(3)
    x_hop("m")
    z_hop2(2)
    z_hop4(1)
    x_hop("f")
    z_hop3(2)
    x_hop("p")
    z_hop2(3)
    y_hop(2, "n")
    up(1, block_at(1, 0))
    up(0, block_at(0, 1))
    x_last("f")
    x_last("m")
    z_hop4(2)
    up(0, block_at(0, 0))
    x_last("p")
    y_hop(2, "t")
    z_hop3(3)
    up(2, block_at(2, 0))
    y_last(0)
    up(0, block_at(0, 3))
    up(0, block_at(0, 2))
    core_last()
    y_hop(1, "f")
    take_fragment()
    y_hop(2, "f")
    y_hop(3, "t")
    y_last(2)
    z_hop4(3)
    y_hop(3, "n")
    up(3, block_at(3, 1))
    cot_in.wait()
    in_part(0)
    y_last(1)
    up(2, block_at(2, 3))
    up(2, block_at(2, 1))
    up(1, block_at(1, 2))
    up(3, block_at(3, 0))
    in_part(1)
    in_part(2)
    up(1, block_at(1, 1))
    up(1, block_at(1, 3))
    y_hop(3, "f")
    y_last(3)
    up(3, block_at(3, 2))
    up(2, block_at(2, 2))
    up(3, block_at(3, 3))
    in_relay(1)
    out_start(0)
    in_relay(0)
    out_start(1)
    out_own()
    in_part(3)
    out_reduce()
    in_sum()
    in_place()
    down(1)
    out_relay()
    out_sum()
    down(0)
    down(3)
    in_result()
    down(2)
    out_result()
    in_spread()
    in_spread_more()
    out_spread()
    out_last()
    in_last()

    stores = [load(FIN, fin_hbm), load(FOUT, fout_hbm)]
    C.flush()
    for copy in stores:
        copy.wait()
    for copy in mix_out:
        copy.wait()


SCRATCH = [
    ((4, 256, 1024), BF),
    ((4, 4, 1024, 256), BF),
    ((4, 4, 1024, 256), BF),
    ((512, 1024), BF),
    ((512, 1024), BF),
    ((512, 1024), BF),
    ((1024, 512), BF),
    ((4, 512, 1024), BF),
    ((4, 512, 256), F32),
    ((4, 512, 256), BF),
    ((1024, 256), F32),
    ((3, 1024, 256), BF),
    ((6, 512, 256), BF),
    ((1024, 256), BF),
    ((7, 128, 256), BF),
    ((4, 2, 128, 256), BF),
    ((2, 2, 256, 1024), F32),
    ((2, 256, 1024), F32),
    ((256, 512), BF),
    ((128, 1024), F32),
    ((3, 128, 1024), BF),
    ((6, 64, 1024), BF),
    ((4, 128, 256), BF),
    ((3, 128, 256), BF),
    ((2, 4, 128, 256), BF),
    ((512, 1024), BF),
    ((4, 1024, 256), BF),
    ((512, 1024), BF),
    ((4, 512, 1024), BF),
]


def path_step(frag_index, tokens, cotangent, w_in, w_out):
    anywhere = pl.BlockSpec(memory_space=pl.ANY)
    return pl.pallas_call(
        kernel,
        out_shape=(
            jax.ShapeDtypeStruct((1, 1, 512, 1024), BF),
            jax.ShapeDtypeStruct((4, 2, 128, 256), BF),
            jax.ShapeDtypeStruct((2, 4, 128, 256), BF),
        ),
        in_specs=[pl.BlockSpec(memory_space=pltpu.SMEM)] + [anywhere] * 4,
        out_specs=(anywhere,) * 3,
        scratch_shapes=[pltpu.VMEM(shape, dtype) for shape, dtype in SCRATCH]
        + [pltpu.SemaphoreType.DMA((180,)), pltpu.SemaphoreType.DMA((180,)), pltpu.SemaphoreType.DMA((20,))],
        compiler_params=pltpu.CompilerParams(
            collective_id=0, has_side_effects=True, vmem_limit_bytes=60 * 2**20
        ),
        cost_estimate=pl.CostEstimate(flops=12 * 2**30, bytes_accessed=24 * 2**20, transcendentals=2**21),
        name="path_step",
    )(frag_index, tokens, cotangent, w_in, w_out)


def outer_kernel(
    frag, mix_hbm, sin_hbm, sout_hbm, win_hbm, wout_hbm, min_hbm, mout_hbm,
    mixed, new_in, new_mom_in, new_out, new_mom_out,
    SIN, SOUT, WI, WO, MI, MO, NI, NMI, NO, NMO, sems,
):
    start_in = pl.multiple_of(frag[lax.axis_index("row")] * FU, FU)
    start_out = pl.multiple_of(frag[lax.axis_size("row") + lax.axis_index("col")] * FU, FU)
    begun = []

    def move(src, dst):
        copy = pltpu.make_async_copy(src, dst, sems.at[len(begun)])
        copy.start()
        begun.append(copy)
        return copy

    first = [move(min_hbm.at[0], MI), move(win_hbm.at[0, :, pl.ds(start_in, FU)], WI), move(sin_hbm, SIN)]
    second = [move(mout_hbm.at[0], MO), move(wout_hbm.at[0, pl.ds(start_out, FU), :], WO), move(sout_hbm, SOUT)]
    last = [move(mix_hbm, mixed)]

    def update(delta, mom, frag_now):
        delta = INNER_LR * delta.astype(F32)
        mom = MOMENTUM * mom + delta
        return mom, (frag_now.astype(F32) - OUTER_LR * (delta + MOMENTUM * mom)).astype(BF)

    for copy in first:
        copy.wait()
    for u in range(4):
        for h in range(2):
            at = (slice(h * 128, h * 128 + 128), slice(u * 256, u * 256 + 256))
            NMI[at], NI[at] = update(SIN[u, h], MI[at], WI[at])
    last += [move(NMI, new_mom_in.at[0]), move(NI, new_in.at[0])]
    for copy in second:
        copy.wait()
    for h in range(2):
        for o in range(4):
            at = slice(h * 512 + o * 128, h * 512 + o * 128 + 128)
            NMO[at, :], NO[at, :] = update(SOUT[h, o], MO[at, :], WO[at, :])
    last += [move(NMO, new_mom_out.at[0]), move(NO, new_out.at[0])]
    for copy in last:
        copy.wait()


def shards(tokens, cotangent, w_in, w_out, frag_index, mom_in, mom_out):
    mixed, sums_in, sums_out = path_step(frag_index, tokens, cotangent, w_in, w_out)
    anywhere = pl.BlockSpec(memory_space=pl.ANY)
    sizes = [
        ((4, 2, 128, 256), BF), ((2, 4, 128, 256), BF), ((256, FU), BF), ((FU, 256), BF), ((256, FU), F32),
        ((FU, 256), F32), ((256, FU), BF), ((256, FU), F32), ((FU, 256), BF), ((FU, 256), F32),
    ]
    return pl.pallas_call(
        outer_kernel,
        out_shape=(
            jax.ShapeDtypeStruct((1, 1, 512, 1024), BF),
            jax.ShapeDtypeStruct((1, 256, FU), BF),
            jax.ShapeDtypeStruct((1, 256, FU), F32),
            jax.ShapeDtypeStruct((1, FU, 256), BF),
            jax.ShapeDtypeStruct((1, FU, 256), F32),
        ),
        in_specs=[pl.BlockSpec(memory_space=pltpu.SMEM)] + [anywhere] * 7,
        out_specs=(anywhere,) * 5,
        scratch_shapes=[pltpu.VMEM(shape, dtype) for shape, dtype in sizes] + [pltpu.SemaphoreType.DMA((12,))],
        compiler_params=pltpu.CompilerParams(vmem_limit_bytes=60 * 2**20),
        cost_estimate=pl.CostEstimate(flops=2**22, bytes_accessed=9 * 2**20, transcendentals=0),
        name="outer_update",
    )(frag_index, mixed, sums_in, sums_out, w_in, w_out, mom_in, mom_out)


def solution(mesh):
    placed = (
        P("row", "col", "shard", None),
        P("row", "col", "shard", None),
        P("row", "shard", None),
        P("col", None, "shard"),
        P(),
        P("row", "shard", None),
        P("col", None, "shard"),
    )
    return jax.shard_map(
        shards,
        mesh=mesh,
        in_specs=placed,
        out_specs=(
            P("row", "col", "shard", None),
            P("row", "shard", None),
            P("row", "shard", None),
            P("col", None, "shard"),
            P("col", None, "shard"),
        ),
        check_vma=False,
    )
```

```python
import jax
import jax.numpy as jnp
from jax import lax
from jax.experimental import pallas as pl
from jax.experimental.pallas import tpu as pltpu
from jax.sharding import PartitionSpec as P

MESH = pl.DeviceIdType.MESH
BF, F32 = jnp.bfloat16, jnp.float32
FU = 1024
EPS = 1e-06
INNER_LR = 0.05
MOMENTUM = 0.9
OUTER_LR = 0.7
GELU_SCALE = 0.7978845608028654
GELU_CUBIC = 0.044715
DOUBLE = (False, False, True, True)


class Place:
    def __init__(p):
        p.r, p.c, p.s = lax.axis_index("row"), lax.axis_index("col"), lax.axis_index("shard")
        p.x, p.k, p.y, p.l = p.r // 2, p.r % 2, p.c // 2, p.c % 2
        p.turn = 2 * p.l - 1

    def near(p):
        return (p.r, p.y * 2 + 1 - p.l, (p.s + p.turn + 4) % 4)

    def twin(p):
        return (p.r, p.y * 2 + 1 - p.l, p.s)

    def at_y(p, d):
        return (p.r, ((p.y + d + 4) % 4) * 2 + p.l, p.s)

    def twin_y(p, d):
        return (p.r, ((p.y + d + 4) % 4) * 2 + 1 - p.l, p.s)

    def at_x(p, d):
        return (((p.x + d + 4) % 4) * 2 + p.k, p.c, p.s)

    def at_s(p, d):
        return (p.r, p.c, (p.s + d + 4) % 4)

    def twin_s(p, d):
        return (p.r, p.y * 2 + 1 - p.l, (p.s + d + 4) % 4)

    def sib(p):
        return (p.x * 2 + 1 - p.k, p.c, p.s)

    def partners(p):
        some = [p.twin(), p.sib()]
        some += [p.at_y(d) for d in (1, 2, 3)] + [p.at_x(d) for d in (1, 2, 3)] + [p.at_s(d) for d in (1, 2, 3)]
        some += [p.twin_s(d) for d in (1, 2, 3)]
        return some


class Copies:
    def __init__(self, send, recv):
        self.send, self.recv, self.sent, self.ids = send, recv, [], {}

    def at(self, name):
        return self.recv.at[self.ids.setdefault(name, len(self.ids))]

    def put(self, name, src, dst, dev):
        copy = pltpu.make_async_remote_copy(
            src_ref=src, dst_ref=dst, send_sem=self.send.at[len(self.sent)], recv_sem=self.at(name),
            device_id=dev, device_id_type=MESH,
        )
        copy.start()
        self.sent.append(copy)
        return copy

    def got(self, name, slot):
        pltpu.make_async_remote_copy(
            src_ref=slot, dst_ref=slot, send_sem=self.send.at[0], recv_sem=self.at(name),
            device_id=self.sent[0].device_id, device_id_type=MESH,
        ).wait_recv()

    def flush(self):
        for copy in self.sent:
            copy.wait_send()


def gelu(v):
    tangent = jnp.tanh(GELU_SCALE * (v + GELU_CUBIC * v * v * v))
    return tangent, 0.5 * v * (1.0 + tangent)


def slope_of(v, tangent):
    return 0.5 * (1.0 + tangent) + 0.5 * v * (1.0 - tangent * tangent) * GELU_SCALE * (
        1.0 + 3.0 * GELU_CUBIC * v * v
    )


def rows(start, size):
    return pl.ds(pl.multiple_of(start, size), size)


def kernel(
    frag, tok_hbm, cot_hbm, win_hbm, wout_hbm,
    mix_hbm, fin_hbm, fout_hbm,
    OWN, WIN, WOUT, TOK, COT, NORM, NT, HID, SLOPE, PG, GIF, GIB, RA, RB, RBR, FIN,
    GO, GOR, HT, GXF, GXB, RX, RSB, RSR, FOUT, MIX, WFRAG, HFRAG, HIDN,
    send, recv, local,
):
    p = Place()
    C = Copies(send, recv)
    y, s, r, x, k, l = p.y, p.s, p.r, p.x, p.k, p.l
    yp, ym, yf = (y + 1) % 4, (y + 3) % 4, (y + 2) % 4
    ci = frag[r]
    ej = frag[8 + p.c]
    te = lax.rem(ej - ci + 4, 4)
    quarter = [lax.rem(ci + t, 4) for t in range(4)]
    turned = [lax.rem(q - ci + 4, 4) for q in range(4)]

    fetch, mix_out = [], []

    def load(src, dst):
        copy = pltpu.make_async_copy(src, dst, local.at[len(fetch)])
        copy.start()
        fetch.append(copy)
        return copy

    own_in = [load(win_hbm.at[0, :, pl.ds(q * 1024, 1024)], OWN.at[q]) for q in range(4)]
    tok_in = load(tok_hbm.at[0, 0], TOK)
    cot_in = load(cot_hbm.at[0, 0], COT)
    wout_in = [load(wout_hbm.at[0, pl.ds(q * 1024, 1024), :], WOUT.at[s, q]) for q in range(4)]

    barrier = pltpu.get_barrier_semaphore()
    partners = p.partners()
    for dev in partners:
        pl.semaphore_signal(barrier, inc=1, device_id=dev, device_id_type=MESH)
    pl.semaphore_wait(barrier, len(partners))

    near, twin, sib = p.near(), p.twin(), p.sib()
    shard = {"n": (s + p.turn + 4) % 4, "t": (s - p.turn + 4) % 4, "f": (s + 2) % 4}
    so = {"m": (s + 3) % 4, "p": (s + 1) % 4, "f": (s + 2) % 4}
    ox = {"0": r, "m": ((x + 3) % 4) * 2 + k, "p": ((x + 1) % 4) * 2 + k, "f": ((x + 2) % 4) * 2 + k}

    def wo(f, o, g=None):
        if g is None:
            return WOUT.at[f, o // 2, rows((o % 2) * 512, 512), :]
        return WOUT.at[f, o // 2, rows((o % 2) * 512 + g * 256, 256), :]

    def s_start():
        mine = wout_hbm.at[0, rows(r * 512, 512), :]
        C.put("s1m", mine, wo(s, r), p.at_s(1))
        C.put("s1p", mine, wo(s, r), p.at_s(-1))

    def s_hop(side):
        if side == "m":
            C.got("s1m", wo(so["m"], r))
            ref = wo(so["m"], r, 0)
            C.put("s2m", ref, ref, p.at_s(1))
        else:
            C.got("s1p", wo(so["p"], r))
            ref = wo(so["p"], r, 1)
            C.put("s2p", ref, ref, p.at_s(-1))

    def s_last():
        C.got("s2m", wo(so["f"], r, 0))
        C.got("s2p", wo(so["f"], r, 1))

    def x_send(f):
        ref = wo(so[f], r)
        C.put(f"xm{f}", ref, ref, p.at_x(1))
        C.put(f"xp{f}", ref, ref, p.at_x(-1))
        C.put(f"c0{f}", ref, ref, sib)

    def x_hop(f):
        a, b = wo(so[f], ox["m"]), wo(so[f], ox["p"])
        C.got(f"xm{f}", a)
        ref = wo(so[f], ox["m"], 0)
        C.put(f"vm{f}", ref, ref, p.at_x(1))
        C.got(f"xp{f}", b)
        ref = wo(so[f], ox["p"], 1)
        C.put(f"vp{f}", ref, ref, p.at_x(-1))
        C.put(f"cm{f}", a, a, sib)
        C.put(f"cp{f}", b, b, sib)

    def x_last(f):
        C.got(f"vm{f}", wo(so[f], ox["f"], 0))
        C.got(f"vp{f}", wo(so[f], ox["f"], 1))
        ref = wo(so[f], ox["f"])
        C.put(f"cf{f}", ref, ref, sib)

    def core_last():
        for copy in wout_in:
            copy.wait()
        for f in "mpf":
            for o, at in ox.items():
                C.got(f"c{o}{f}", wo(so[f], at + 1 - 2 * k))

    first, second = l, 1 - l

    def zc(t, f, h):
        if DOUBLE[t]:
            return WIN.at[t, y % 2 + 2 * h, rows(f * 256, 256), :]
        return WIN.at[t, y, rows(f * 256 + h * 128, 128), :]

    def z_start(t):
        ref = zc(t, s, first)
        C.put(f"z{t}nB", ref, ref, near)
        ref = zc(t, s, second)
        C.put(f"z{t}nA", ref, ref, near)

    def z_hop1(t):
        ref = zc(t, shard["n"], first)
        C.got(f"z{t}nA", ref)
        C.put(f"z{t}tB", ref, ref, twin)
        ref = zc(t, shard["n"], second)
        C.got(f"z{t}nB", ref)
        C.put(f"z{t}tA", ref, ref, twin)
        y_send(t, "n")

    def z_hop2(t):
        ref = zc(t, shard["t"], second)
        C.got(f"z{t}tB", ref)
        C.put(f"z{t}fA", ref, ref, near)
        C.got(f"z{t}tA", zc(t, shard["t"], first))
        y_send(t, "t")

    def z_hop3(t):
        ref = zc(t, shard["f"], first)
        C.got(f"z{t}fA", ref)
        C.put(f"z{t}fB", ref, ref, twin)

    def z_hop4(t):
        C.got(f"z{t}fB", zc(t, shard["f"], second))
        y_send(t, "f")

    def blk(t, u, f, h=None):
        if h is None:
            return WIN.at[t, u, rows(shard[f] * 256, 256), :]
        return WIN.at[t, u, rows(shard[f] * 256 + h * 128, 128), :]

    def from_m(t):
        return (y + 1) % 2 if DOUBLE[t] else ym

    def from_p(t):
        return (y + 1) % 2 + 2 if DOUBLE[t] else yp

    def y_send(t, f):
        a = blk(t, y % 2 if DOUBLE[t] else y, f)
        b = blk(t, y % 2 + 2 if DOUBLE[t] else y, f)
        C.put(f"y{t}{f}m", a, a, p.at_y(1))
        C.put(f"y{t}{f}p", b, b, p.at_y(-1))

    def y_hop(t, f):
        C.got(f"y{t}{f}m", blk(t, from_m(t), f))
        if not DOUBLE[t]:
            ref = blk(t, ym, f, 0)
            C.put(f"w{t}{f}m", ref, ref, p.at_y(1))
        C.got(f"y{t}{f}p", blk(t, from_p(t), f))
        if not DOUBLE[t]:
            ref = blk(t, yp, f, 1)
            C.put(f"w{t}{f}p", ref, ref, p.at_y(-1))

    def y_last(t):
        if not DOUBLE[t]:
            for f in "ntf":
                C.got(f"w{t}{f}m", blk(t, yf, f, 0))
                C.got(f"w{t}{f}p", blk(t, yf, f, 1))

    def place_own(t):
        block = OWN[quarter[t]]
        for u in range(4):
            WIN[t, u, rows(s * 256, 256), :] = block[:, u * 256 : u * 256 + 256]

    def normalize():
        tok_in.wait()

        @pl.loop(0, 8)
        def _(i):
            at = rows(i * 64, 64)
            stream = TOK[at, :].astype(F32)
            mean = jnp.mean(stream * stream, axis=-1, keepdims=True)
            NORM[at, :] = (stream * lax.rsqrt(mean + EPS)).astype(BF)

    def transpose_normed():
        for i in range(4):
            NT[:, i * 128 : i * 128 + 128] = NORM[i * 128 : i * 128 + 128, :].T

    def up(t, u):
        @pl.loop(0, 2)
        def _(i):
            at = rows(i * 256, 256)
            v = jnp.dot(NORM[at, :], WIN[t, u], preferred_element_type=F32)
            tangent, value = gelu(v)
            HID[t, at, rows(u * 256, 256)] = value.astype(BF)
            if t == 0:
                SLOPE[u, at, :] = slope_of(v, tangent)

    def block_at(t, n):
        if DOUBLE[t]:
            return (y % 2, y % 2 + 2, (y + 1) % 2, (y + 1) % 2 + 2)[n]
        return (y, ym, yp, yf)[n]

    def take_fragment():
        for b in range(4):
            WFRAG[b] = WOUT[b, ci]

    def pre_grad(u):
        @pl.loop(0, 2)
        def _(i):
            at = rows(i * 256, 256)
            total = jnp.zeros((256, 256), F32)
            for b in range(4):
                total += lax.dot_general(
                    COT[at, b * 256 : b * 256 + 256],
                    WFRAG[b, rows(u * 256, 256), :],
                    (((1,), (1,)), ((), ())),
                    preferred_element_type=F32,
                )
            PG[u, at, :] = (total * SLOPE[u, at, :]).astype(BF)

    def grad_in(u, out):
        @pl.loop(0, 4)
        def _(i):
            at = rows(i * 256, 256)
            out[at, :] = jnp.dot(NT[at, :], PG[u], preferred_element_type=F32).astype(out.dtype)

    LO, HI = pl.ds(0, 512), pl.ds(512, 512)

    def in_part(n):
        u = (yf, yp, ym, y)[n]
        pre_grad(u)
        grad_in(u, (GIB.at[2], GIB.at[0], GIB.at[1], GIF)[n])
        if n == 0:
            C.put("ai0", GIB.at[2, LO], RA.at[0], p.at_y(1))
            C.put("ai1", GIB.at[2, HI], RA.at[1], p.at_y(-1))
        if n == 1:
            C.put("ai2", GIB.at[0, HI], RA.at[2], p.at_y(1))
        if n == 2:
            C.put("ai3", GIB.at[1, LO], RA.at[3], p.at_y(-1))

    def in_relay(side):
        if side == 0:
            C.got("ai0", RA.at[0])
            GIB[0, LO, :] = (GIB[0, LO, :].astype(F32) + RA[0].astype(F32)).astype(BF)
            C.put("ai4", GIB.at[0, LO], RA.at[4], p.at_y(1))
        else:
            C.got("ai1", RA.at[1])
            GIB[1, HI, :] = (GIB[1, HI, :].astype(F32) + RA[1].astype(F32)).astype(BF)
            C.put("ai5", GIB.at[1, HI], RA.at[5], p.at_y(-1))

    zs = [(d, e) for d in range(4) for e in range(2) if (d, e) != (0, 0)]

    def in_sum():
        C.got("ai2", RA.at[2])
        C.got("ai3", RA.at[3])
        C.got("ai4", RA.at[4])
        C.got("ai5", RA.at[5])
        RB[LO, :] = (GIF[LO, :] + RA[3].astype(F32) + RA[4].astype(F32)).astype(BF)
        RB[HI, :] = (GIF[HI, :] + RA[2].astype(F32) + RA[5].astype(F32)).astype(BF)
        for n, (d, e) in enumerate(zs):
            piece = rows(((s + d) % 4) * 256 + (l + e - 2 * l * e) * 128, 128)
            dev = p.at_s(d) if e == 0 else p.twin_s(d)
            C.put(f"bi{n}", RB.at[piece], RBR.at[n], dev)

    def in_result():
        total = RB[rows(s * 256 + l * 128, 128), :].astype(F32)
        for n in range(7):
            C.got(f"bi{n}", RBR.at[n])
            total += RBR[n].astype(F32)
        FIN[y, l] = total.astype(BF)
        ref = FIN.at[y, l]
        C.put("ct", ref, ref, twin)
        C.put("cm0", ref, ref, p.at_y(1))
        C.put("cp0", ref, ref, p.at_y(-1))

    def in_spread():
        other = FIN.at[y, 1 - l]
        C.got("ct", other)
        C.put("cm1", other, other, p.at_y(1))
        C.put("cp1", other, other, p.at_y(-1))

    def in_spread_more():
        C.got("cm0", FIN.at[ym, l])
        ref = FIN.at[ym, l]
        C.put("cf0", ref, ref, p.at_y(1))
        C.got("cp1", FIN.at[yp, 1 - l])
        ref = FIN.at[yp, 1 - l]
        C.put("cf1", ref, ref, p.at_y(-1))
        C.got("cp0", FIN.at[yp, l])
        C.got("cm1", FIN.at[ym, 1 - l])

    def in_last():
        C.got("cf0", FIN.at[yf, l])
        C.got("cf1", FIN.at[yf, 1 - l])

    def grad_out(half, v, out):
        HT[...] = HFRAG[:, rows((half * 2 + v) * 256, 256)].T

        @pl.loop(0, 4)
        def _(i):
            at = rows(i * 256, 256)
            out[v, :, at] = jnp.dot(HT[...], COT[:, at], preferred_element_type=F32)

    def in_place():
        for q in range(4):
            HIDN[q] = HID[turned[q]]

    def out_start(v):
        if v == 0:
            HFRAG[...] = HID[te]
        grad_out(1 - k, v, GO.at[1])
        C.put(f"g{v}", GO.at[1, v], GOR.at[v], sib)

    def out_own():
        for v in range(2):
            grad_out(k, v, GO.at[0])

    def part(d):
        o = (x + d) % 4
        return o // 2, rows((o % 2) * 128, 128)

    def out_reduce():
        C.got("g0", GOR.at[0])
        C.got("g1", GOR.at[1])
        for slot, d in ((2, 2), (0, 1), (1, 3), (None, 0)):
            b, at = part(d)
            total = GO[0, b, at, :] + GOR[b, at, :]
            if slot is None:
                GXF[...] = total
            else:
                GXB[slot] = total.astype(BF)
            if slot == 2:
                C.put("gx0", GXB.at[2, pl.ds(0, 64)], RX.at[0], p.at_x(1))
                C.put("gx1", GXB.at[2, pl.ds(64, 64)], RX.at[1], p.at_x(-1))
            if slot == 0:
                C.put("gx2", GXB.at[0, pl.ds(64, 64)], RX.at[2], p.at_x(1))
            if slot == 1:
                C.put("gx3", GXB.at[1, pl.ds(0, 64)], RX.at[3], p.at_x(-1))

    def out_relay():
        C.got("gx0", RX.at[0])
        GXB[0, 0:64, :] = (GXB[0, 0:64, :].astype(F32) + RX[0].astype(F32)).astype(BF)
        C.put("gx4", GXB.at[0, pl.ds(0, 64)], RX.at[4], p.at_x(1))
        C.got("gx1", RX.at[1])
        GXB[1, 64:128, :] = (GXB[1, 64:128, :].astype(F32) + RX[1].astype(F32)).astype(BF)
        C.put("gx5", GXB.at[1, pl.ds(64, 64)], RX.at[5], p.at_x(-1))

    def out_sum():
        for n in (2, 3, 4, 5):
            C.got(f"gx{n}", RX.at[n])
        for b in range(4):
            at = pl.ds(b * 256, 256)
            RSB[b, 0:64, :] = (GXF[0:64, at] + RX[3, :, at].astype(F32) + RX[4, :, at].astype(F32)).astype(BF)
            RSB[b, 64:128, :] = (GXF[64:128, at] + RX[2, :, at].astype(F32) + RX[5, :, at].astype(F32)).astype(BF)
        for d in (2, 1, 3):
            C.put(f"gs{d}", RSB.at[(s + d) % 4], RSR.at[d - 1], p.at_s(d))

    def out_result():
        total = RSB[s].astype(F32)
        for d in (1, 2, 3):
            C.got(f"gs{d}", RSR.at[d - 1])
            total += RSR[d - 1].astype(F32)
        FOUT[k, x] = total.astype(BF)
        ref = FOUT.at[k, x]
        C.put("hm", ref, ref, p.at_x(1))
        C.put("hp", ref, ref, p.at_x(-1))
        C.put("hf", ref, ref, p.at_x(2))
        C.put("h0", ref, ref, sib)

    def out_spread():
        for n, d in (("m", 3), ("p", 1), ("f", 2)):
            ref = FOUT.at[k, (x + d) % 4]
            C.got("h" + n, ref)
            C.put("i" + n, ref, ref, sib)

    def out_last():
        for n, d in (("h0", 0), ("im", 3), ("ip", 1), ("if", 2)):
            C.got(n, FOUT.at[1 - k, (x + d) % 4])

    def down(b):
        @pl.loop(0, 2)
        def _(i):
            at = rows(i * 256, 256)
            total = TOK[at, b * 256 : b * 256 + 256].astype(F32)
            for t in range(4):
                total += jnp.dot(
                    HIDN[t, at, :], WOUT[b, t], preferred_element_type=F32
                )
            MIX[at, b * 256 : b * 256 + 256] = total.astype(BF)

        mix_out.append(load(MIX.at[:, pl.ds(b * 256, 256)], mix_hbm.at[0, 0, :, pl.ds(b * 256, 256)]))

    s_start()
    for copy in own_in:
        copy.wait()
    place_own(0)
    z_start(0)
    place_own(1)
    z_hop1(0)
    z_start(1)
    z_hop2(0)
    place_own(2)
    z_start(2)
    z_hop1(1)
    normalize()
    z_hop3(0)
    s_hop("m")
    x_send("m")
    z_hop2(1)
    y_hop(0, "t")
    y_hop(0, "n")
    s_hop("p")
    z_hop4(0)
    x_send("p")
    place_own(3)
    transpose_normed()
    y_hop(1, "t")
    y_hop(1, "n")
    z_start(3)
    z_hop1(2)
    s_last()
    x_send("f")
    z_hop3(1)
    y_hop(0, "f")
    z_hop1(3)
    x_hop("m")
    z_hop2(2)
    z_hop4(1)
    x_hop("f")
    z_hop3(2)
    x_hop("p")
    z_hop2(3)
    y_hop(2, "n")
    up(1, block_at(1, 0))
    up(0, block_at(0, 1))
    x_last("f")
    x_last("m")
    z_hop4(2)
    up(0, block_at(0, 0))
    x_last("p")
    y_hop(2, "t")
    z_hop3(3)
    up(2, block_at(2, 0))
    y_last(0)
    up(0, block_at(0, 3))
    up(0, block_at(0, 2))
    core_last()
    y_hop(1, "f")
    take_fragment()
    y_hop(2, "f")
    y_hop(3, "t")
    y_last(2)
    z_hop4(3)
    y_hop(3, "n")
    up(3, block_at(3, 1))
    cot_in.wait()
    in_part(0)
    y_last(1)
    up(2, block_at(2, 3))
    up(2, block_at(2, 1))
    up(1, block_at(1, 2))
    up(3, block_at(3, 0))
    in_part(1)
    in_part(2)
    up(1, block_at(1, 1))
    up(1, block_at(1, 3))
    y_hop(3, "f")
    y_last(3)
    up(3, block_at(3, 2))
    up(2, block_at(2, 2))
    up(3, block_at(3, 3))
    in_relay(1)
    out_start(0)
    in_relay(0)
    out_start(1)
    out_own()
    in_part(3)
    out_reduce()
    in_sum()
    in_place()
    down(1)
    out_relay()
    out_sum()
    down(0)
    down(3)
    in_result()
    down(2)
    out_result()
    in_spread()
    in_spread_more()
    out_spread()
    out_last()
    in_last()

    stores = [load(FIN, fin_hbm), load(FOUT, fout_hbm)]
    C.flush()
    for copy in stores:
        copy.wait()
    for copy in mix_out:
        copy.wait()


SCRATCH = [
    ((4, 256, 1024), BF),
    ((4, 4, 1024, 256), BF),
    ((4, 4, 1024, 256), BF),
    ((512, 1024), BF),
    ((512, 1024), BF),
    ((512, 1024), BF),
    ((1024, 512), BF),
    ((4, 512, 1024), BF),
    ((4, 512, 256), F32),
    ((4, 512, 256), BF),
    ((1024, 256), F32),
    ((3, 1024, 256), BF),
    ((6, 512, 256), BF),
    ((1024, 256), BF),
    ((7, 128, 256), BF),
    ((4, 2, 128, 256), BF),
    ((2, 2, 256, 1024), F32),
    ((2, 256, 1024), F32),
    ((256, 512), BF),
    ((128, 1024), F32),
    ((3, 128, 1024), BF),
    ((6, 64, 1024), BF),
    ((4, 128, 256), BF),
    ((3, 128, 256), BF),
    ((2, 4, 128, 256), BF),
    ((512, 1024), BF),
    ((4, 1024, 256), BF),
    ((512, 1024), BF),
    ((4, 512, 1024), BF),
]


def path_step(frag_index, tokens, cotangent, w_in, w_out):
    anywhere = pl.BlockSpec(memory_space=pl.ANY)
    return pl.pallas_call(
        kernel,
        out_shape=(
            jax.ShapeDtypeStruct((1, 1, 512, 1024), BF),
            jax.ShapeDtypeStruct((4, 2, 128, 256), BF),
            jax.ShapeDtypeStruct((2, 4, 128, 256), BF),
        ),
        in_specs=[pl.BlockSpec(memory_space=pltpu.SMEM)] + [anywhere] * 4,
        out_specs=(anywhere,) * 3,
        scratch_shapes=[pltpu.VMEM(shape, dtype) for shape, dtype in SCRATCH]
        + [pltpu.SemaphoreType.DMA((180,)), pltpu.SemaphoreType.DMA((180,)), pltpu.SemaphoreType.DMA((20,))],
        compiler_params=pltpu.CompilerParams(
            collective_id=0, has_side_effects=True, vmem_limit_bytes=60 * 2**20
        ),
        cost_estimate=pl.CostEstimate(flops=12 * 2**30, bytes_accessed=24 * 2**20, transcendentals=2**21),
        name="path_step",
    )(frag_index, tokens, cotangent, w_in, w_out)


def outer_kernel(
    frag, mix_hbm, sin_hbm, sout_hbm, win_hbm, wout_hbm, min_hbm, mout_hbm,
    mixed, new_in, new_mom_in, new_out, new_mom_out,
    SIN, SOUT, WI, WO, MI, MO, NI, NMI, NO, NMO, MX, sems,
):
    start_in = pl.multiple_of(frag[lax.axis_index("row")] * FU, FU)
    start_out = pl.multiple_of(frag[lax.axis_size("row") + lax.axis_index("col")] * FU, FU)
    begun = []

    def move(src, dst):
        copy = pltpu.make_async_copy(src, dst, sems.at[len(begun)])
        copy.start()
        begun.append(copy)
        return copy

    first = [move(min_hbm.at[0], MI), move(win_hbm.at[0, :, pl.ds(start_in, FU)], WI), move(sin_hbm, SIN)]
    second = [move(mout_hbm.at[0], MO), move(wout_hbm.at[0, pl.ds(start_out, FU), :], WO), move(sout_hbm, SOUT)]
    window = move(mix_hbm, MX)
    last = []

    def update(delta, mom, frag_now):
        delta = INNER_LR * delta.astype(F32)
        mom = MOMENTUM * mom + delta
        return mom, (frag_now.astype(F32) - OUTER_LR * (delta + MOMENTUM * mom)).astype(BF)

    for copy in first:
        copy.wait()
    for u in range(4):
        for h in range(2):
            at = (slice(h * 128, h * 128 + 128), slice(u * 256, u * 256 + 256))
            NMI[at], NI[at] = update(SIN[u, h], MI[at], WI[at])
    last += [move(NMI, new_mom_in.at[0]), move(NI, new_in.at[0])]
    window.wait()
    last.append(move(MX, mixed))
    for copy in second:
        copy.wait()
    for h in range(2):
        for o in range(4):
            at = slice(h * 512 + o * 128, h * 512 + o * 128 + 128)
            NMO[at, :], NO[at, :] = update(SOUT[h, o], MO[at, :], WO[at, :])
    last += [move(NMO, new_mom_out.at[0]), move(NO, new_out.at[0])]
    for copy in last:
        copy.wait()


def shards(tokens, cotangent, w_in, w_out, frag_index, mom_in, mom_out):
    mixed, sums_in, sums_out = path_step(frag_index, tokens, cotangent, w_in, w_out)
    anywhere = pl.BlockSpec(memory_space=pl.ANY)
    sizes = [
        ((4, 2, 128, 256), BF), ((2, 4, 128, 256), BF), ((256, FU), BF), ((FU, 256), BF), ((256, FU), F32),
        ((FU, 256), F32), ((256, FU), BF), ((256, FU), F32), ((FU, 256), BF), ((FU, 256), F32), ((1, 1, 512, 1024), BF),
    ]
    return pl.pallas_call(
        outer_kernel,
        out_shape=(
            jax.ShapeDtypeStruct((1, 1, 512, 1024), BF),
            jax.ShapeDtypeStruct((1, 256, FU), BF),
            jax.ShapeDtypeStruct((1, 256, FU), F32),
            jax.ShapeDtypeStruct((1, FU, 256), BF),
            jax.ShapeDtypeStruct((1, FU, 256), F32),
        ),
        in_specs=[pl.BlockSpec(memory_space=pltpu.SMEM)] + [anywhere] * 7,
        out_specs=(anywhere,) * 5,
        scratch_shapes=[pltpu.VMEM(shape, dtype) for shape, dtype in sizes] + [pltpu.SemaphoreType.DMA((12,))],
        compiler_params=pltpu.CompilerParams(vmem_limit_bytes=60 * 2**20),
        cost_estimate=pl.CostEstimate(flops=2**22, bytes_accessed=9 * 2**20, transcendentals=0),
        name="outer_update",
    )(frag_index, mixed, sums_in, sums_out, w_in, w_out, mom_in, mom_out)


def solution(mesh):
    placed = (
        P("row", "col", "shard", None),
        P("row", "col", "shard", None),
        P("row", "shard", None),
        P("col", None, "shard"),
        P(),
        P("row", "shard", None),
        P("col", None, "shard"),
    )
    return jax.shard_map(
        shards,
        mesh=mesh,
        in_specs=placed,
        out_specs=(
            P("row", "col", "shard", None),
            P("row", "shard", None),
            P("row", "shard", None),
            P("col", None, "shard"),
            P("col", None, "shard"),
        ),
        check_vma=False,
    )
```

```python
import jax
import jax.numpy as jnp
from jax import lax
from jax.experimental import pallas as pl
from jax.experimental.pallas import tpu as pltpu
from jax.sharding import PartitionSpec as P

MESH = pl.DeviceIdType.MESH
BF, F32 = jnp.bfloat16, jnp.float32
FU = 1024
EPS = 1e-06
INNER_LR = 0.05
MOMENTUM = 0.9
OUTER_LR = 0.7
GELU_SCALE = 0.7978845608028654
GELU_CUBIC = 0.044715
DOUBLE = (False, False, True, True)


class Place:
    def __init__(p):
        p.r, p.c, p.s = lax.axis_index("row"), lax.axis_index("col"), lax.axis_index("shard")
        p.x, p.k, p.y, p.l = p.r // 2, p.r % 2, p.c // 2, p.c % 2
        p.turn = 2 * p.l - 1

    def near(p):
        return (p.r, p.y * 2 + 1 - p.l, (p.s + p.turn + 4) % 4)

    def twin(p):
        return (p.r, p.y * 2 + 1 - p.l, p.s)

    def at_y(p, d):
        return (p.r, ((p.y + d + 4) % 4) * 2 + p.l, p.s)

    def twin_y(p, d):
        return (p.r, ((p.y + d + 4) % 4) * 2 + 1 - p.l, p.s)

    def at_x(p, d):
        return (((p.x + d + 4) % 4) * 2 + p.k, p.c, p.s)

    def at_s(p, d):
        return (p.r, p.c, (p.s + d + 4) % 4)

    def twin_s(p, d):
        return (p.r, p.y * 2 + 1 - p.l, (p.s + d + 4) % 4)

    def sib(p):
        return (p.x * 2 + 1 - p.k, p.c, p.s)

    def partners(p):
        some = [p.twin(), p.sib()]
        some += [p.at_y(d) for d in (1, 2, 3)] + [p.at_x(d) for d in (1, 2, 3)] + [p.at_s(d) for d in (1, 2, 3)]
        some += [p.twin_s(d) for d in (1, 2, 3)]
        return some


class Copies:
    def __init__(self, send, recv):
        self.send, self.recv, self.sent, self.ids, self.flushed = send, recv, [], {}, 0

    def at(self, name):
        return self.recv.at[self.ids.setdefault(name, len(self.ids))]

    def put(self, name, src, dst, dev):
        copy = pltpu.make_async_remote_copy(
            src_ref=src, dst_ref=dst, send_sem=self.send.at[len(self.sent)], recv_sem=self.at(name),
            device_id=dev, device_id_type=MESH,
        )
        copy.start()
        self.sent.append(copy)
        return copy

    def got(self, name, slot):
        pltpu.make_async_remote_copy(
            src_ref=slot, dst_ref=slot, send_sem=self.send.at[0], recv_sem=self.at(name),
            device_id=self.sent[0].device_id, device_id_type=MESH,
        ).wait_recv()

    def flush(self, end):
        for copy in self.sent[self.flushed : end]:
            copy.wait_send()
        self.flushed = end


def gelu(v):
    tangent = jnp.tanh(GELU_SCALE * (v + GELU_CUBIC * v * v * v))
    return tangent, 0.5 * v * (1.0 + tangent)


def slope_of(v, tangent):
    return 0.5 * (1.0 + tangent) + 0.5 * v * (1.0 - tangent * tangent) * GELU_SCALE * (
        1.0 + 3.0 * GELU_CUBIC * v * v
    )


def rows(start, size):
    return pl.ds(pl.multiple_of(start, size), size)


def kernel(
    frag, tok_hbm, cot_hbm, win_hbm, wout_hbm,
    mix_hbm, fin_hbm, fout_hbm,
    OWN, WIN, WOUT, TOK, COT, NORM, NT, HID, SLOPE, PG, GIF, GIB, RA, RB, RBR, FIN,
    GO, GOR, HT, GXF, GXB, RX, RSB, RSR, FOUT, MIX, WFRAG, HFRAG, HIDN,
    send, recv, local,
):
    p = Place()
    C = Copies(send, recv)
    y, s, r, x, k, l = p.y, p.s, p.r, p.x, p.k, p.l
    yp, ym, yf = (y + 1) % 4, (y + 3) % 4, (y + 2) % 4
    ci = frag[r]
    ej = frag[8 + p.c]
    te = lax.rem(ej - ci + 4, 4)
    quarter = [lax.rem(ci + t, 4) for t in range(4)]
    turned = [lax.rem(q - ci + 4, 4) for q in range(4)]

    fetch, mix_out = [], []

    def load(src, dst):
        copy = pltpu.make_async_copy(src, dst, local.at[len(fetch)])
        copy.start()
        fetch.append(copy)
        return copy

    own_in = [load(win_hbm.at[0, :, pl.ds(q * 1024, 1024)], OWN.at[q]) for q in range(4)]
    tok_in = load(tok_hbm.at[0, 0], TOK)
    cot_in = load(cot_hbm.at[0, 0], COT)
    wout_in = [load(wout_hbm.at[0, pl.ds(q * 1024, 1024), :], WOUT.at[s, q]) for q in range(4)]

    barrier = pltpu.get_barrier_semaphore()
    partners = p.partners()
    for dev in partners:
        pl.semaphore_signal(barrier, inc=1, device_id=dev, device_id_type=MESH)

    near, twin, sib = p.near(), p.twin(), p.sib()
    shard = {"n": (s + p.turn + 4) % 4, "t": (s - p.turn + 4) % 4, "f": (s + 2) % 4}
    so = {"m": (s + 3) % 4, "p": (s + 1) % 4, "f": (s + 2) % 4}
    ox = {"0": r, "m": ((x + 3) % 4) * 2 + k, "p": ((x + 1) % 4) * 2 + k, "f": ((x + 2) % 4) * 2 + k}

    def wo(f, o, g=None):
        if g is None:
            return WOUT.at[f, o // 2, rows((o % 2) * 512, 512), :]
        return WOUT.at[f, o // 2, rows((o % 2) * 512 + g * 256, 256), :]

    mine = wout_hbm.at[0, rows(r * 512, 512), :]

    def s_start(side):
        C.put(f"s1{side}", mine, wo(s, r), p.at_s(1 if side == "m" else -1))

    def s_hop(side):
        if side == "m":
            C.got("s1m", wo(so["m"], r))
            ref = wo(so["m"], r, 0)
            C.put("s2m", ref, ref, p.at_s(1))
        else:
            C.got("s1p", wo(so["p"], r))
            ref = wo(so["p"], r, 1)
            C.put("s2p", ref, ref, p.at_s(-1))

    def s_last():
        C.got("s2m", wo(so["f"], r, 0))
        C.got("s2p", wo(so["f"], r, 1))

    def x_send(f):
        ref = wo(so[f], r)
        C.put(f"xm{f}", ref, ref, p.at_x(1))
        C.put(f"xp{f}", ref, ref, p.at_x(-1))
        C.put(f"c0{f}", ref, ref, sib)

    def x_hop(side, f):
        a = wo(so[f], ox[side])
        C.got(f"x{side}{f}", a)
        ref = wo(so[f], ox[side], 0 if side == "m" else 1)
        C.put(f"v{side}{f}", ref, ref, p.at_x(1 if side == "m" else -1))
        C.put(f"c{side}{f}", a, a, sib)

    def x_last(f):
        C.got(f"vm{f}", wo(so[f], ox["f"], 0))
        C.got(f"vp{f}", wo(so[f], ox["f"], 1))
        ref = wo(so[f], ox["f"])
        C.put(f"cf{f}", ref, ref, sib)

    def core_last():
        for copy in wout_in:
            copy.wait()
        for f in "mpf":
            for o, at in ox.items():
                C.got(f"c{o}{f}", wo(so[f], at + 1 - 2 * k))

    first, second = l, 1 - l

    def zc(t, f, h):
        if DOUBLE[t]:
            return WIN.at[t, y % 2 + 2 * h, rows(f * 256, 256), :]
        return WIN.at[t, y, rows(f * 256 + h * 128, 128), :]

    def z_start(t):
        ref = zc(t, s, first)
        C.put(f"z{t}nB", ref, ref, near)
        ref = zc(t, s, second)
        C.put(f"z{t}nA", ref, ref, near)

    def z_hop1(t, role):
        ref = zc(t, shard["n"], first if role == "A" else second)
        C.got(f"z{t}n{role}", ref)
        C.put(f"z{t}t" + ("B" if role == "A" else "A"), ref, ref, twin)

    def z_hop2(t):
        ref = zc(t, shard["t"], second)
        C.got(f"z{t}tB", ref)
        C.put(f"z{t}fA", ref, ref, near)

    def z_hop3(t):
        ref = zc(t, shard["f"], first)
        C.got(f"z{t}fA", ref)
        C.put(f"z{t}fB", ref, ref, twin)

    def blk(t, u, f, h=None):
        if h is None:
            return WIN.at[t, u, rows(shard[f] * 256, 256), :]
        return WIN.at[t, u, rows(shard[f] * 256 + h * 128, 128), :]

    def from_m(t):
        return (y + 1) % 2 if DOUBLE[t] else ym

    def from_p(t):
        return (y + 1) % 2 + 2 if DOUBLE[t] else yp

    def y_send(t, f):
        if f == "t":
            C.got(f"z{t}tA", zc(t, shard["t"], first))
        if f == "f":
            C.got(f"z{t}fB", zc(t, shard["f"], second))
        a = blk(t, y % 2 if DOUBLE[t] else y, f)
        b = blk(t, y % 2 + 2 if DOUBLE[t] else y, f)
        C.put(f"y{t}{f}m", a, a, p.at_y(1))
        C.put(f"y{t}{f}p", b, b, p.at_y(-1))

    def y_hop(side, t, f):
        at, h = (ym, 0) if side == "m" else (yp, 1)
        C.got(f"y{t}{f}{side}", blk(t, from_m(t) if side == "m" else from_p(t), f))
        if not DOUBLE[t]:
            ref = blk(t, at, f, h)
            C.put(f"w{t}{f}{side}", ref, ref, p.at_y(1 if side == "m" else -1))

    def y_last(t):
        if not DOUBLE[t]:
            for f in "ntf":
                C.got(f"w{t}{f}m", blk(t, yf, f, 0))
                C.got(f"w{t}{f}p", blk(t, yf, f, 1))

    def place_own(t):
        block = OWN[quarter[t]]
        for u in range(4):
            WIN[t, u, rows(s * 256, 256), :] = block[:, u * 256 : u * 256 + 256]

    def normalize():
        tok_in.wait()

        @pl.loop(0, 8)
        def _(i):
            at = rows(i * 64, 64)
            stream = TOK[at, :].astype(F32)
            mean = jnp.mean(stream * stream, axis=-1, keepdims=True)
            NORM[at, :] = (stream * lax.rsqrt(mean + EPS)).astype(BF)

    def transpose_normed():
        for i in range(4):
            NT[:, i * 128 : i * 128 + 128] = NORM[i * 128 : i * 128 + 128, :].T

    def up(t, u):
        @pl.loop(0, 2)
        def _(i):
            at = rows(i * 256, 256)
            v = jnp.dot(NORM[at, :], WIN[t, u], preferred_element_type=F32)
            tangent, value = gelu(v)
            HID[t, at, rows(u * 256, 256)] = value.astype(BF)
            if t == 0:
                SLOPE[u, at, :] = slope_of(v, tangent)

    def block_at(t, n):
        if DOUBLE[t]:
            return (y % 2, y % 2 + 2, (y + 1) % 2, (y + 1) % 2 + 2)[n]
        return (y, ym, yp, yf)[n]

    def take_fragment():
        for b in range(4):
            WFRAG[b] = WOUT[b, ci]

    def pre_grad(u):
        @pl.loop(0, 2)
        def _(i):
            at = rows(i * 256, 256)
            total = jnp.zeros((256, 256), F32)
            for b in range(4):
                total += lax.dot_general(
                    COT[at, b * 256 : b * 256 + 256],
                    WFRAG[b, rows(u * 256, 256), :],
                    (((1,), (1,)), ((), ())),
                    preferred_element_type=F32,
                )
            PG[u, at, :] = (total * SLOPE[u, at, :]).astype(BF)

    def grad_in(u, out):
        @pl.loop(0, 4)
        def _(i):
            at = rows(i * 256, 256)
            out[at, :] = jnp.dot(NT[at, :], PG[u], preferred_element_type=F32).astype(out.dtype)

    LO, HI = pl.ds(0, 512), pl.ds(512, 512)

    def in_part(n):
        u = (yf, yp, ym, y)[n]
        pre_grad(u)
        grad_in(u, (GIB.at[2], GIB.at[0], GIB.at[1], GIF)[n])
        if n == 0:
            C.put("ai0", GIB.at[2, LO], RA.at[0], p.at_y(1))
            C.put("ai1", GIB.at[2, HI], RA.at[1], p.at_y(-1))
        if n == 1:
            C.put("ai2", GIB.at[0, HI], RA.at[2], p.at_y(1))
        if n == 2:
            C.put("ai3", GIB.at[1, LO], RA.at[3], p.at_y(-1))

    def in_relay(side):
        if side == 0:
            C.got("ai0", RA.at[0])
            GIB[0, LO, :] = (GIB[0, LO, :].astype(F32) + RA[0].astype(F32)).astype(BF)
            C.put("ai4", GIB.at[0, LO], RA.at[4], p.at_y(1))
        else:
            C.got("ai1", RA.at[1])
            GIB[1, HI, :] = (GIB[1, HI, :].astype(F32) + RA[1].astype(F32)).astype(BF)
            C.put("ai5", GIB.at[1, HI], RA.at[5], p.at_y(-1))

    zs = [(2, 0), (2, 1), (1, 1), (3, 1), (1, 0), (3, 0), (0, 1)]

    def in_sum():
        C.got("ai2", RA.at[2])
        C.got("ai3", RA.at[3])
        C.got("ai4", RA.at[4])
        C.got("ai5", RA.at[5])
        RB[LO, :] = (GIF[LO, :] + RA[3].astype(F32) + RA[4].astype(F32)).astype(BF)
        RB[HI, :] = (GIF[HI, :] + RA[2].astype(F32) + RA[5].astype(F32)).astype(BF)
        for n, (d, e) in enumerate(zs):
            piece = rows(((s + d) % 4) * 256 + (l + e - 2 * l * e) * 128, 128)
            dev = p.at_s(d) if e == 0 else p.twin_s(d)
            C.put(f"bi{n}", RB.at[piece], RBR.at[n], dev)

    def in_result():
        total = RB[rows(s * 256 + l * 128, 128), :].astype(F32)
        for n in range(7):
            C.got(f"bi{n}", RBR.at[n])
            total += RBR[n].astype(F32)
        FIN[y, l] = total.astype(BF)
        ref = FIN.at[y, l]
        C.put("ct", ref, ref, twin)
        C.put("cm0", ref, ref, p.at_y(1))
        C.put("cp0", ref, ref, p.at_y(-1))

    def in_spread():
        other = FIN.at[y, 1 - l]
        C.got("ct", other)
        C.put("cm1", other, other, p.at_y(1))
        C.put("cp1", other, other, p.at_y(-1))

    def in_spread_more():
        C.got("cm0", FIN.at[ym, l])
        ref = FIN.at[ym, l]
        C.put("cf0", ref, ref, p.at_y(1))
        C.got("cp1", FIN.at[yp, 1 - l])
        ref = FIN.at[yp, 1 - l]
        C.put("cf1", ref, ref, p.at_y(-1))
        C.got("cp0", FIN.at[yp, l])
        C.got("cm1", FIN.at[ym, 1 - l])

    def in_last():
        C.got("cf0", FIN.at[yf, l])
        C.got("cf1", FIN.at[yf, 1 - l])

    def grad_out(half, v, out):
        HT[...] = HFRAG[:, rows((half * 2 + v) * 256, 256)].T

        @pl.loop(0, 4)
        def _(i):
            at = rows(i * 256, 256)
            out[v, :, at] = jnp.dot(HT[...], COT[:, at], preferred_element_type=F32)

    def in_place():
        for q in range(4):
            HIDN[q] = HID[turned[q]]

    def out_start(v):
        if v == 0:
            HFRAG[...] = HID[te]
        grad_out(1 - k, v, GO.at[1])
        C.put(f"g{v}", GO.at[1, v], GOR.at[v], sib)

    def out_own():
        for v in range(2):
            grad_out(k, v, GO.at[0])

    def part(d):
        o = (x + d) % 4
        return o // 2, rows((o % 2) * 128, 128)

    def out_reduce():
        C.got("g0", GOR.at[0])
        C.got("g1", GOR.at[1])
        for slot, d in ((2, 2), (0, 1), (1, 3), (None, 0)):
            b, at = part(d)
            total = GO[0, b, at, :] + GOR[b, at, :]
            if slot is None:
                GXF[...] = total
            else:
                GXB[slot] = total.astype(BF)
            if slot == 2:
                C.put("gx0", GXB.at[2, pl.ds(0, 64)], RX.at[0], p.at_x(1))
                C.put("gx1", GXB.at[2, pl.ds(64, 64)], RX.at[1], p.at_x(-1))
            if slot == 0:
                C.put("gx2", GXB.at[0, pl.ds(64, 64)], RX.at[2], p.at_x(1))
            if slot == 1:
                C.put("gx3", GXB.at[1, pl.ds(0, 64)], RX.at[3], p.at_x(-1))

    def out_relay():
        C.got("gx0", RX.at[0])
        GXB[0, 0:64, :] = (GXB[0, 0:64, :].astype(F32) + RX[0].astype(F32)).astype(BF)
        C.put("gx4", GXB.at[0, pl.ds(0, 64)], RX.at[4], p.at_x(1))
        C.got("gx1", RX.at[1])
        GXB[1, 64:128, :] = (GXB[1, 64:128, :].astype(F32) + RX[1].astype(F32)).astype(BF)
        C.put("gx5", GXB.at[1, pl.ds(64, 64)], RX.at[5], p.at_x(-1))

    def out_sum():
        for n in (2, 3, 4, 5):
            C.got(f"gx{n}", RX.at[n])
        for b in range(4):
            at = pl.ds(b * 256, 256)
            RSB[b, 0:64, :] = (GXF[0:64, at] + RX[3, :, at].astype(F32) + RX[4, :, at].astype(F32)).astype(BF)
            RSB[b, 64:128, :] = (GXF[64:128, at] + RX[2, :, at].astype(F32) + RX[5, :, at].astype(F32)).astype(BF)
        for d in (2, 1, 3):
            C.put(f"gs{d}", RSB.at[(s + d) % 4], RSR.at[d - 1], p.at_s(d))

    def out_result():
        total = RSB[s].astype(F32)
        for d in (1, 2, 3):
            C.got(f"gs{d}", RSR.at[d - 1])
            total += RSR[d - 1].astype(F32)
        FOUT[k, x] = total.astype(BF)
        ref = FOUT.at[k, x]
        C.put("hm", ref, ref, p.at_x(1))
        C.put("hp", ref, ref, p.at_x(-1))
        C.put("hf", ref, ref, p.at_x(2))
        C.put("h0", ref, ref, sib)

    def out_spread():
        for n, d in (("m", 3), ("p", 1), ("f", 2)):
            ref = FOUT.at[k, (x + d) % 4]
            C.got("h" + n, ref)
            C.put("i" + n, ref, ref, sib)

    def out_last():
        for n, d in (("h0", 0), ("im", 3), ("ip", 1), ("if", 2)):
            C.got(n, FOUT.at[1 - k, (x + d) % 4])

    def down(b):
        @pl.loop(0, 2)
        def _(i):
            at = rows(i * 256, 256)
            total = TOK[at, b * 256 : b * 256 + 256].astype(F32)
            for t in range(4):
                total += jnp.dot(
                    HIDN[t, at, :], WOUT[b, t], preferred_element_type=F32
                )
            MIX[at, b * 256 : b * 256 + 256] = total.astype(BF)

        mix_out.append(load(MIX.at[:, pl.ds(b * 256, 256)], mix_hbm.at[0, 0, :, pl.ds(b * 256, 256)]))

    for copy in own_in:
        copy.wait()
    place_own(0)
    place_own(1)
    pl.semaphore_wait(barrier, len(partners))
    s_start("m")
    s_start("p")
    z_start(0)
    z_hop1(0, "A")
    z_hop1(0, "B")
    y_send(0, "n")
    z_start(1)
    z_hop2(0)
    y_send(0, "t")
    place_own(2)
    z_start(2)
    z_hop1(1, "A")
    z_hop1(1, "B")
    y_send(1, "n")
    normalize()
    z_hop3(0)
    s_hop("m")
    x_send("m")
    z_hop2(1)
    y_send(1, "t")
    y_hop("m", 0, "t")
    y_hop("p", 0, "t")
    y_hop("m", 0, "n")
    y_hop("p", 0, "n")
    s_hop("p")
    y_send(0, "f")
    x_send("p")
    place_own(3)
    transpose_normed()
    y_hop("m", 1, "t")
    y_hop("p", 1, "t")
    y_hop("m", 1, "n")
    y_hop("p", 1, "n")
    z_start(3)
    z_hop1(2, "A")
    z_hop1(2, "B")
    y_send(2, "n")
    s_last()
    x_send("f")
    z_hop3(1)
    y_hop("m", 0, "f")
    y_hop("p", 0, "f")
    z_hop1(3, "A")
    z_hop1(3, "B")
    y_send(3, "n")
    x_hop("m", "m")
    x_hop("p", "m")
    z_hop2(2)
    y_send(2, "t")
    y_send(1, "f")
    x_hop("m", "f")
    x_hop("p", "f")
    z_hop3(2)
    x_hop("m", "p")
    x_hop("p", "p")
    z_hop2(3)
    y_send(3, "t")
    y_hop("m", 2, "n")
    y_hop("p", 2, "n")
    up(1, block_at(1, 0))
    up(0, block_at(0, 1))
    x_last("f")
    x_last("m")
    y_send(2, "f")
    up(0, block_at(0, 0))
    x_last("p")
    y_hop("m", 2, "t")
    y_hop("p", 2, "t")
    z_hop3(3)
    up(2, block_at(2, 0))
    y_last(0)
    up(0, block_at(0, 3))
    up(0, block_at(0, 2))
    core_last()
    y_hop("m", 1, "f")
    y_hop("p", 1, "f")
    take_fragment()
    y_hop("m", 2, "f")
    y_hop("p", 2, "f")
    y_hop("m", 3, "t")
    y_hop("p", 3, "t")
    y_last(2)
    y_send(3, "f")
    y_hop("m", 3, "n")
    y_hop("p", 3, "n")
    up(3, block_at(3, 1))
    cot_in.wait()
    in_part(0)
    y_last(1)
    up(2, block_at(2, 3))
    up(2, block_at(2, 1))
    up(1, block_at(1, 2))
    up(3, block_at(3, 0))
    in_part(1)
    in_part(2)
    up(1, block_at(1, 1))
    up(1, block_at(1, 3))
    y_hop("m", 3, "f")
    y_hop("p", 3, "f")
    y_last(3)
    up(3, block_at(3, 2))
    up(2, block_at(2, 2))
    up(3, block_at(3, 3))
    in_relay(1)
    gathered = len(C.sent)
    out_start(0)
    in_relay(0)
    out_start(1)
    out_own()
    in_part(3)
    out_reduce()
    in_sum()
    in_place()
    C.flush(gathered)
    down(1)
    out_relay()
    out_sum()
    down(0)
    down(3)
    in_result()
    down(2)
    out_result()
    in_spread()
    in_spread_more()
    out_spread()
    out_last()
    in_last()
    stores = [load(FIN, fin_hbm)]

    stores.append(load(FOUT, fout_hbm))
    C.flush(len(C.sent))
    for copy in stores:
        copy.wait()
    for copy in mix_out:
        copy.wait()


SCRATCH = [
    ((4, 256, 1024), BF),
    ((4, 4, 1024, 256), BF),
    ((4, 4, 1024, 256), BF),
    ((512, 1024), BF),
    ((512, 1024), BF),
    ((512, 1024), BF),
    ((1024, 512), BF),
    ((4, 512, 1024), BF),
    ((4, 512, 256), F32),
    ((4, 512, 256), BF),
    ((1024, 256), F32),
    ((3, 1024, 256), BF),
    ((6, 512, 256), BF),
    ((1024, 256), BF),
    ((7, 128, 256), BF),
    ((4, 2, 128, 256), BF),
    ((2, 2, 256, 1024), F32),
    ((2, 256, 1024), F32),
    ((256, 512), BF),
    ((128, 1024), F32),
    ((3, 128, 1024), BF),
    ((6, 64, 1024), BF),
    ((4, 128, 256), BF),
    ((3, 128, 256), BF),
    ((2, 4, 128, 256), BF),
    ((512, 1024), BF),
    ((4, 1024, 256), BF),
    ((512, 1024), BF),
    ((4, 512, 1024), BF),
]


def path_step(frag_index, tokens, cotangent, w_in, w_out):
    anywhere = pl.BlockSpec(memory_space=pl.ANY)
    return pl.pallas_call(
        kernel,
        out_shape=(
            jax.ShapeDtypeStruct((1, 1, 512, 1024), BF),
            jax.ShapeDtypeStruct((4, 2, 128, 256), BF),
            jax.ShapeDtypeStruct((2, 4, 128, 256), BF),
        ),
        in_specs=[pl.BlockSpec(memory_space=pltpu.SMEM)] + [anywhere] * 4,
        out_specs=(anywhere,) * 3,
        scratch_shapes=[pltpu.VMEM(shape, dtype) for shape, dtype in SCRATCH]
        + [pltpu.SemaphoreType.DMA((180,)), pltpu.SemaphoreType.DMA((180,)), pltpu.SemaphoreType.DMA((20,))],
        compiler_params=pltpu.CompilerParams(
            collective_id=0, has_side_effects=True, vmem_limit_bytes=60 * 2**20
        ),
        cost_estimate=pl.CostEstimate(flops=12 * 2**30, bytes_accessed=24 * 2**20, transcendentals=2**21),
        name="path_step",
    )(frag_index, tokens, cotangent, w_in, w_out)


def outer_kernel(
    frag, mix_hbm, sin_hbm, sout_hbm, win_hbm, wout_hbm, min_hbm, mout_hbm,
    mixed, new_in, new_mom_in, new_out, new_mom_out,
    SIN, SOUT, WI, WO, MI, MO, NI, NMI, NO, NMO, MX, sems,
):
    start_in = pl.multiple_of(frag[lax.axis_index("row")] * FU, FU)
    start_out = pl.multiple_of(frag[lax.axis_size("row") + lax.axis_index("col")] * FU, FU)
    begun = []

    def move(src, dst):
        copy = pltpu.make_async_copy(src, dst, sems.at[len(begun)])
        copy.start()
        begun.append(copy)
        return copy

    first = [move(min_hbm.at[0], MI), move(win_hbm.at[0, :, pl.ds(start_in, FU)], WI), move(sin_hbm, SIN)]
    second = [move(mout_hbm.at[0], MO), move(wout_hbm.at[0, pl.ds(start_out, FU), :], WO), move(sout_hbm, SOUT)]
    window = move(mix_hbm, MX)
    last = []

    def update(delta, mom, frag_now):
        delta = INNER_LR * delta.astype(F32)
        mom = MOMENTUM * mom + delta
        return mom, (frag_now.astype(F32) - OUTER_LR * (delta + MOMENTUM * mom)).astype(BF)

    for copy in first:
        copy.wait()
    for u in range(4):
        for h in range(2):
            at = (slice(h * 128, h * 128 + 128), slice(u * 256, u * 256 + 256))
            NMI[at], NI[at] = update(SIN[u, h], MI[at], WI[at])
    last += [move(NMI, new_mom_in.at[0]), move(NI, new_in.at[0])]
    window.wait()
    last.append(move(MX, mixed))
    for copy in second:
        copy.wait()
    for h in range(2):
        for o in range(4):
            at = slice(h * 512 + o * 128, h * 512 + o * 128 + 128)
            NMO[at, :], NO[at, :] = update(SOUT[h, o], MO[at, :], WO[at, :])
    last += [move(NMO, new_mom_out.at[0]), move(NO, new_out.at[0])]
    for copy in last:
        copy.wait()


def shards(tokens, cotangent, w_in, w_out, frag_index, mom_in, mom_out):
    mixed, sums_in, sums_out = path_step(frag_index, tokens, cotangent, w_in, w_out)
    anywhere = pl.BlockSpec(memory_space=pl.ANY)
    sizes = [
        ((4, 2, 128, 256), BF), ((2, 4, 128, 256), BF), ((256, FU), BF), ((FU, 256), BF), ((256, FU), F32),
        ((FU, 256), F32), ((256, FU), BF), ((256, FU), F32), ((FU, 256), BF), ((FU, 256), F32), ((1, 1, 512, 1024), BF),
    ]
    return pl.pallas_call(
        outer_kernel,
        out_shape=(
            jax.ShapeDtypeStruct((1, 1, 512, 1024), BF),
            jax.ShapeDtypeStruct((1, 256, FU), BF),
            jax.ShapeDtypeStruct((1, 256, FU), F32),
            jax.ShapeDtypeStruct((1, FU, 256), BF),
            jax.ShapeDtypeStruct((1, FU, 256), F32),
        ),
        in_specs=[pl.BlockSpec(memory_space=pltpu.SMEM)] + [anywhere] * 7,
        out_specs=(anywhere,) * 5,
        scratch_shapes=[pltpu.VMEM(shape, dtype) for shape, dtype in sizes] + [pltpu.SemaphoreType.DMA((12,))],
        compiler_params=pltpu.CompilerParams(vmem_limit_bytes=60 * 2**20),
        cost_estimate=pl.CostEstimate(flops=2**22, bytes_accessed=9 * 2**20, transcendentals=0),
        name="outer_update",
    )(frag_index, mixed, sums_in, sums_out, w_in, w_out, mom_in, mom_out)


def solution(mesh):
    placed = (
        P("row", "col", "shard", None),
        P("row", "col", "shard", None),
        P("row", "shard", None),
        P("col", None, "shard"),
        P(),
        P("row", "shard", None),
        P("col", None, "shard"),
    )
    return jax.shard_map(
        shards,
        mesh=mesh,
        in_specs=placed,
        out_specs=(
            P("row", "col", "shard", None),
            P("row", "shard", None),
            P("row", "shard", None),
            P("col", None, "shard"),
            P("col", None, "shard"),
        ),
        check_vma=False,
    )
```
